32 devices in a mesh: rows: 8 (over z, x), cols: 4 (over y, core).
Axes of the slice: x: 2, y: 2, z: 4, core: 2. Of those that a mesh axis runs over, the one named last changes fastest.
Arguments:
- column_lists: int32 [32, 13], replicated, may hold values from -1 to 31, as said below
- block_values: bfloat16 [32, 13, 128, 128], P('rows'), as said below
Outputs:
- purified: bfloat16 [32, 13, 128, 128], P('rows', None, None, 'cols')
The draws below stay inside these ranges and needn't reach their ends.
Inputs may be any that keep to these rules, and one draw needn't show every extreme that they name: `column_lists`: slot (13 - 1) // 2 of row i holds i. Slot s of row i holds -1 or a row j, and then slot 12 - s of row j holds i. There is an ordering of the rows, taken cyclically, in which the row in slot s of row i stands s - (13 - 1) // 2 places after row i. With owners the aligned groups of 4 rows, the slots of one owner's rows hold at most 2 rows of any one other owner, and some pair of owners has exactly 2. Over the slots s of one owner's rows that hold rows of one other owner, the sum of 13 - |s - (13 - 1) // 2| is at most 16, and exactly 16 for some pair of owners. block_values[j, 12 - s] is the transpose of block_values[i, s] where slot s of row i holds j; blocks of empty slots are zero.
All inputs are finite; a program needn't handle non-finite values.
Results may differ from the reference program's by a relative error of at most 0.0039.
Values may be sent and summed in bfloat16 or wider, within the bound.
A program may use at most 128 MiB of HBM per device.

```python
import jax
import jax.numpy as jnp
from jax import lax

BLK = 128
SLOTS = 13
CAP = 2
BAND = 16
RB_DEV = 4
NB = 32
N_ROWS = 8


def pattern_tables(key):
    all_rows = RB_DEV * N_ROWS
    middle = (SLOTS - 1) // 2
    key_owner, key_order, key_keep = jax.random.split(key, 3)
    owners = jax.random.permutation(key_owner, N_ROWS).astype(jnp.int32)
    first_owner = owners[0]
    second_owner = owners[1]
    chosen = jnp.stack([first_owner * RB_DEV, second_owner * RB_DEV, second_owner * RB_DEV + 1]).astype(jnp.int32)
    scores = jax.random.permutation(key_order, all_rows).astype(jnp.int32)
    scores = scores.at[chosen].set(jnp.arange(3, dtype=jnp.int32) - 3)
    first_order = jnp.argsort(scores, stable=True).astype(jnp.int32)
    ordering = jnp.concatenate([first_order[0:1], first_order[3:6], first_order[1:2], first_order[6:7], first_order[2:3], first_order[7:]])
    place = jnp.arange(all_rows, dtype=jnp.int32)[:, None]
    offset = jnp.arange(1, middle + 1, dtype=jnp.int32)[None, :]
    left_row = jnp.broadcast_to(ordering[:, None], (all_rows, middle))
    right_row = ordering[(place + offset) % all_rows]
    rate_left = (4 * all_rows - 2 * left_row) * 64 // (4 * all_rows)
    rate_right = (4 * all_rows - 2 * right_row) * 64 // (4 * all_rows)
    keep_level = rate_left * rate_right // 64
    ticket = jax.random.randint(key_keep, (all_rows, middle), 0, 64).astype(jnp.int32)
    forced = (place == 0) & ((offset == 4) | (offset == 6))
    wanted = forced | (ticket < keep_level) & (place != 0)
    owner_left = left_row // RB_DEV
    owner_right = right_row // RB_DEV
    crossing = owner_left != owner_right
    pair_key = jnp.minimum(owner_left, owner_right) * N_ROWS + jnp.maximum(owner_left, owner_right)
    keyed = jnp.where(wanted & crossing, pair_key, N_ROWS * N_ROWS).reshape(-1).astype(jnp.int32)
    edge_count = all_rows * middle
    sort_order = jnp.argsort(keyed, stable=True).astype(jnp.int32)
    sorted_key = keyed[sort_order]
    positions = jnp.arange(edge_count, dtype=jnp.int32)
    changed = jnp.concatenate([jnp.ones((1,), dtype=bool), sorted_key[1:] != sorted_key[:-1]])
    group_starts = jnp.where(changed, positions, 0)
    group_first = lax.cummax(group_starts, axis=0)
    edge_rank = jnp.zeros((edge_count,), jnp.int32).at[sort_order].set(positions - group_first).reshape(all_rows, middle)
    edge_weight = jnp.broadcast_to(SLOTS - offset, (all_rows, middle)).reshape(-1).astype(jnp.int32)
    sorted_weight = edge_weight[sort_order]
    running_weight = jnp.cumsum(sorted_weight).astype(jnp.int32)
    group_base = running_weight[group_first] - sorted_weight[group_first]
    edge_load = jnp.zeros((edge_count,), jnp.int32).at[sort_order].set(running_weight - group_base).reshape(all_rows, middle)
    kept_edge = wanted & (~crossing | (edge_rank < CAP) & (edge_load <= BAND))
    edge_id = place * middle + offset - 1
    row_ids = jnp.arange(all_rows, dtype=jnp.int32)
    column_table = jnp.full((all_rows, SLOTS), -1, jnp.int32).at[:, middle].set(row_ids)
    column_table = column_table.at[left_row, middle + offset].set(jnp.where(kept_edge, right_row, -1))
    column_table = column_table.at[right_row, middle - offset].set(jnp.where(kept_edge, left_row, -1))
    identity = jnp.full((all_rows, SLOTS), 0, jnp.int32).at[:, middle].set(edge_count + row_ids)
    identity = identity.at[left_row, middle + offset].set(edge_id)
    identity = identity.at[right_row, middle - offset].set(edge_id)
    transposed = jnp.zeros((all_rows, SLOTS), dtype=bool).at[right_row, middle - offset].set(True)
    return (column_table, identity, transposed)


def draw_column_lists(key, part):
    return pattern_tables(jax.random.fold_in(key, 7))[0]


def draw_block_values(key, part):
    column_table, identity, transposed = pattern_tables(jax.random.fold_in(key, 7))
    all_rows = RB_DEV * N_ROWS
    middle = (SLOTS - 1) // 2
    key_vals = jax.random.fold_in(key, 8)
    spread = 0.15

    def one_block(block_id):
        block_key = jax.random.fold_in(key_vals, block_id)
        sampled = jax.random.normal(block_key, (BLK, BLK))
        return sampled

    def one_row(row_index):
        block_ids = identity[row_index]
        flips = transposed[row_index]
        sampled = jax.vmap(one_block)(block_ids)
        sampled = jnp.where(flips[:, None, None], jnp.swapaxes(sampled, 1, 2), sampled)
        symmetric = (sampled + jnp.swapaxes(sampled, 1, 2)) * 0.70710678
        centre = (jnp.arange(SLOTS) == middle)[:, None, None]
        sampled = jnp.where(centre, symmetric, sampled)
        factor = spread * jnp.ones((SLOTS,), jnp.float32)
        sampled = sampled * factor[:, None, None]
        return jnp.where((column_table[row_index] >= 0)[:, None, None], sampled, 0.0)
    return lax.map(one_row, jnp.arange(all_rows, dtype=jnp.int32)).astype(jnp.bfloat16)


def setup_inputs(seed: int = 0) -> dict:
    seeds = jax.random.split(jax.random.key(seed), 3)
    return {
        "column_lists": draw_column_lists(jax.random.fold_in(seeds[2], 71), 0),
        "block_values": draw_block_values(jax.random.fold_in(seeds[2], 71), 0),
    }


def reference(column_lists, block_values):
    present = column_lists >= 0
    target = jnp.maximum(column_lists, 0)
    masked = jnp.where(present[:, :, None, None], block_values, jnp.zeros((), jnp.bfloat16))

    def one_row(row_index):
        own_cols = column_lists[row_index]
        own_present = present[row_index]
        partners = target[row_index]
        partner_blocks = masked[partners].astype(jnp.float32)
        partner_cols = column_lists[partners]
        partner_present = present[partners]
        matches = (partner_cols[:, None, :] == own_cols[None, :, None]) & partner_present[:, None, :]
        matches = matches & own_present[:, None, None] & own_present[None, :, None]
        windows = jnp.einsum("asb,abpq->aspq", matches.astype(jnp.float32), partner_blocks, precision=lax.Precision.HIGHEST)
        own_blocks = masked[row_index].astype(jnp.float32)
        square_sum = jnp.einsum("apq,asqr->spr", own_blocks, windows, precision=lax.Precision.HIGHEST)
        square = jnp.where(own_present[:, None, None], square_sum, 0.0).astype(jnp.bfloat16)
        cube_sum = jnp.einsum("apq,asqr->spr", square.astype(jnp.float32), windows, precision=lax.Precision.HIGHEST)
        purified = jnp.where(own_present[:, None, None], 3.0 * square.astype(jnp.float32) - 2.0 * cube_sum, 0.0)
        return purified.astype(jnp.bfloat16)

    return lax.map(one_row, jnp.arange(NB, dtype=jnp.int32))
```

```python
import functools

import jax
import jax.numpy as jnp
from jax import lax
from jax.experimental import pallas as pl
from jax.experimental.pallas import tpu as pltpu
from jax.sharding import PartitionSpec as P

CAP = 2
BAND = 16
CHUNKS = 3
MESH = pl.DeviceIdType.MESH


def kernel(
    owners, rows, slots, size, strip, band, most,
    cl, blocks, out,
    xt, send, tab, win, own, sq, gat, full,
    owner_of, first_code, first_weight, base_low, base_high, cum, source,
    send_sem, recv_sem, csend_sem, crecv_sem,
):
    middle = (slots - 1) // 2
    last = slots - 1
    count = rows * slots
    me = lax.axis_index("rows")
    part = lax.axis_index("cols")
    high, low = part // 2, part % 2
    sibling = high * 2 + (1 - low)
    across = (1 - high) * 2 + low
    far = (1 - high) * 2 + (1 - low)
    first = me * rows
    local_base = owners * band
    chunk = most // CHUNKS

    def peer_of(j):
        return lax.rem(me + owners // 2 + ((j + 1) // 2) * (1 - 2 * (j % 2)), owners)

    barrier = pltpu.get_barrier_semaphore()

    @pl.loop(0, owners - 1)
    def _(j):
        pl.semaphore_signal(barrier, inc=1, device_id={"rows": peer_of(j)}, device_id_type=MESH)

    for other in (sibling, across):
        pl.semaphore_signal(barrier, inc=1, device_id={"cols": other}, device_id_type=MESH)

    pick = (
        lax.broadcasted_iota(jnp.int32, (strip, size), 1)
        == lax.broadcasted_iota(jnp.int32, (strip, size), 0) + part * strip
    ).astype(jnp.bfloat16)
    zero_block = jnp.zeros((strip, size), jnp.bfloat16)
    xt[count] = zero_block
    sq[count] = zero_block
    for k in range(rows):
        for b in range(slots):
            n = k * slots + b
            column = cl[first + k, b]
            owner_of[n] = jnp.where(column >= 0, jnp.maximum(column, 0) // rows, -1)
            block = blocks[k, b]
            block = jnp.where(column >= 0, block, jnp.zeros_like(block))
            own[k, :, b * size : (b + 1) * size] = block
            strip_t = lax.dot_general(
                pick, block, (((1,), (1,)), ((), ())), preferred_element_type=jnp.float32
            ).astype(jnp.bfloat16)
            xt[n] = strip_t
            tab[local_base + n] = strip_t

    pl.semaphore_wait(barrier, owners - 1 + 2)

    def band_copy(src, dst_owner, peer):
        return pltpu.make_async_remote_copy(
            src_ref=send.at[src],
            dst_ref=tab.at[pl.ds(dst_owner * band, band)],
            send_sem=send_sem.at[src],
            recv_sem=recv_sem.at[dst_owner],
            device_id={"rows": peer},
            device_id_type=MESH,
        )

    @pl.loop(0, owners - 1)
    def _(j):
        peer = peer_of(j)
        lowest = jnp.int32(count)
        highest = jnp.int32(-1)
        for n in range(count):
            hit = owner_of[n] == peer
            lowest = jnp.minimum(lowest, jnp.where(hit, n, count))
            highest = jnp.maximum(highest, jnp.where(hit, n, -1))
        has_one = highest >= 0
        has_two = highest > lowest
        code0 = jnp.where(has_one, lowest, 0)
        code1 = jnp.where(has_two, highest, 0)
        row0, row1 = code0 // slots, code1 // slots
        slot0, slot1 = code0 - row0 * slots, code1 - row1 * slots
        weight0 = jnp.where(has_one, last - jnp.abs(slot0 - middle), 0)
        weight1 = jnp.where(has_two, last - jnp.abs(slot1 - middle), 0)
        start0 = jnp.maximum(slot0 - middle, 0)
        start1 = jnp.maximum(slot1 - middle, 0)
        for u in range(band):
            in0 = u < weight0
            in1 = u < weight0 + weight1
            place = jnp.where(in0, start0 + u, start1 + u - weight0)
            skip = jnp.where(in0, slot0, slot1)
            place = place + jnp.where(place >= skip, 1, 0)
            entry = jnp.where(in0, row0, row1) * slots + place
            entry = jnp.where(in1, entry, count)
            send[peer, u] = xt[entry]
        band_copy(peer, me, peer).start()
        key0 = cl[first + row0, slot0] * slots + last - slot0
        key1 = cl[first + row1, slot1] * slots + last - slot1
        swap = has_two & (key1 < key0)
        first_code[peer] = jnp.where(swap, code1, code0)
        first_weight[peer] = jnp.where(swap, weight1, weight0)

    first_code[me] = 0
    first_weight[me] = 0

    running = jnp.int32(0)
    for i in range(rows):
        for a in range(slots):
            n = i * slots + a
            column = cl[first + i, a]
            running = running + jnp.where(column >= 0, 1, 0)
            cum[n] = running
            column = jnp.where(column >= 0, column, first + i)
            owner = column // rows
            local = owner == me
            begin = max(0, middle - a)
            remote = owner * band + jnp.where(first_code[owner] == n, 0, first_weight[owner])
            here = local_base + (column - first) * slots + begin
            base_low[n] = jnp.where(local, here, remote)
            base_high[n] = jnp.where(local, here + 1, remote)

    @pl.loop(0, most)
    def _(t):
        entry = jnp.int32(0)
        for n in range(count):
            entry = entry + jnp.where(cum[n] <= t, 1, 0)
        source[t] = entry

    @pl.loop(0, rows)
    def _(i):
        for a in range(slots):
            lanes = slice(a * size, (a + 1) * size)
            for s in range(slots):
                b = s - a + middle
                span = slice(s * strip, (s + 1) * strip)
                if b < 0 or b >= slots:
                    win[i, span, lanes] = zero_block
                elif a == middle:
                    win[i, span, lanes] = xt[i * slots + s]
                elif s == middle:
                    win[i, span, lanes] = own[i, pl.ds(pl.multiple_of(part * strip, strip), strip), lanes]

    @pl.loop(0, owners - 1)
    def _(j):
        peer = peer_of(j)
        band_copy(peer, peer, peer).wait_recv()

    @pl.loop(0, rows)
    def _(i):
        for a in range(slots):
            if a == middle:
                continue
            n = i * slots + a
            low_at, high_at = base_low[n], base_high[n]
            begin = max(0, middle - a)
            for s in range(slots):
                b = s - a + middle
                if b < 0 or b >= slots or s == middle:
                    continue
                if s < middle:
                    entry = low_at + (b - begin)
                else:
                    entry = high_at + (b - begin - 1)
                win[i, s * strip : (s + 1) * strip, a * size : (a + 1) * size] = tab[entry]
        total = lax.dot_general(
            win[i], own[i], (((1,), (1,)), ((), ())), preferred_element_type=jnp.float32
        )
        for s in range(slots):
            value = total[s * strip : (s + 1) * strip]
            value = jnp.where(cl[first + i, s] >= 0, value, 0.0)
            sq[i * slots + s] = value.astype(jnp.bfloat16)

    def strip_copy(which, piece, peer, sem):
        span = pl.ds(piece * chunk, chunk)
        return pltpu.make_async_remote_copy(
            src_ref=gat.at[which, span],
            dst_ref=gat.at[which, span],
            send_sem=csend_sem.at[sem, piece],
            recv_sem=crecv_sem.at[sem, piece],
            device_id={"cols": peer},
            device_id_type=MESH,
        )

    for piece in range(CHUNKS):
        for t in range(piece * chunk, (piece + 1) * chunk):
            gat[part, t] = sq[source[t]]
        strip_copy(part, piece, across, 0).start()
        strip_copy(part, piece, sibling, 1).start()
    for piece in range(CHUNKS):
        strip_copy(across, piece, across, 0).wait_recv()
        strip_copy(across, piece, sibling, 2).start()
    for piece in range(CHUNKS):
        strip_copy(sibling, piece, sibling, 1).wait_recv()
    for piece in range(CHUNKS):
        strip_copy(far, piece, sibling, 2).wait_recv()

    @pl.loop(0, rows)
    def _(i):
        for a in range(slots):
            n = i * slots + a
            present = cl[first + i, a] >= 0
            entry = jnp.minimum(jnp.maximum(cum[n] - 1, 0), most - 1)
            for c in range(size // strip):
                value = gat[c, entry]
                value = jnp.where(present, value, jnp.zeros_like(value))
                full[a * size + c * strip : a * size + (c + 1) * strip, :] = value
        total = jnp.dot(win[i], full[...], preferred_element_type=jnp.float32)
        for s in range(slots):
            value = 3.0 * sq[i * slots + s].astype(jnp.float32) - 2.0 * total[s * strip : (s + 1) * strip]
            value = jnp.where(cl[first + i, s] >= 0, value, 0.0)
            out[i, s] = value.astype(jnp.bfloat16)

    @pl.loop(0, owners - 1)
    def _(j):
        peer = peer_of(j)
        band_copy(peer, me, peer).wait_send()

    for piece in range(CHUNKS):
        strip_copy(part, piece, across, 0).wait_send()
        strip_copy(part, piece, sibling, 1).wait_send()
        strip_copy(across, piece, sibling, 2).wait_send()


def body(column_lists, block_values):
    rows, slots, size, _ = block_values.shape
    owners = lax.axis_size("rows")
    parts = lax.axis_size("cols")
    assert parts == 4
    strip = size // parts
    band = BAND - CAP
    count = rows * slots
    most = min(count, rows * rows + CAP * (owners - 1))
    most = -(-most // CHUNKS) * CHUNKS
    bf16 = jnp.bfloat16
    result = pl.pallas_call(
        functools.partial(kernel, owners, rows, slots, size, strip, band, most),
        out_shape=jax.ShapeDtypeStruct((rows, slots, strip, size), bf16),
        in_specs=[
            pl.BlockSpec(memory_space=pltpu.SMEM),
            pl.BlockSpec(memory_space=pltpu.VMEM),
        ],
        out_specs=pl.BlockSpec(memory_space=pltpu.VMEM),
        scratch_shapes=[
            pltpu.VMEM((count + 1, strip, size), bf16),
            pltpu.VMEM((owners, band, strip, size), bf16),
            pltpu.VMEM((owners * band + count, strip, size), bf16),
            pltpu.VMEM((rows, slots * strip, slots * size), bf16),
            pltpu.VMEM((rows, size, slots * size), bf16),
            pltpu.VMEM((count + 1, strip, size), bf16),
            pltpu.VMEM((parts, most, strip, size), bf16),
            pltpu.VMEM((slots * size, size), bf16),
            pltpu.SMEM((count,), jnp.int32),
            pltpu.SMEM((owners,), jnp.int32),
            pltpu.SMEM((owners,), jnp.int32),
            pltpu.SMEM((count,), jnp.int32),
            pltpu.SMEM((count,), jnp.int32),
            pltpu.SMEM((count,), jnp.int32),
            pltpu.SMEM((most,), jnp.int32),
            pltpu.SemaphoreType.DMA((owners,)),
            pltpu.SemaphoreType.DMA((owners,)),
            pltpu.SemaphoreType.DMA((3, CHUNKS)),
            pltpu.SemaphoreType.DMA((3, CHUNKS)),
        ],
        compiler_params=pltpu.CompilerParams(
            collective_id=0, has_side_effects=True, vmem_limit_bytes=48 * 1024 * 1024
        ),
    )(column_lists, block_values)
    return jnp.swapaxes(result, 2, 3)


def solution(mesh):
    in_specs = (P(), P("rows", None, None, None))
    out_specs = P("rows", None, None, "cols")
    return jax.shard_map(body, mesh=mesh, in_specs=in_specs, out_specs=out_specs, check_vma=False)
```

```python
import functools

import jax
import jax.numpy as jnp
from jax import lax
from jax.experimental import pallas as pl
from jax.experimental.pallas import tpu as pltpu
from jax.sharding import PartitionSpec as P

CAP = 2
CHUNKS = 3
MESH = pl.DeviceIdType.MESH


def sends(offset, other):
    if (offset > 0) == (other > 0):
        return abs(other) >= abs(offset)
    return abs(other) < abs(offset) or (abs(other) == abs(offset) and offset > 0)


def kernel(
    owners, rows, slots, size, strip, band, pad, most,
    cl_hbm, blocks_hbm, out,
    cl, blocks, loc, send, tab, win, own, sq, gat, full, turned, pieces, joined, shuffle,
    owner_of, first_code, first_weight, remote_base, local_base, is_local, entries, cum, source,
    send_sem, recv_sem, xsend_sem, xrecv_sem, csend_sem, crecv_sem, in_sem,
):
    middle = (slots - 1) // 2
    count = rows * slots
    parts = size // strip
    me = lax.axis_index("rows")
    part = lax.axis_index("cols")
    high, low = part // 2, part % 2
    sibling = high * 2 + (1 - low)
    across = (1 - high) * 2 + low
    far = (1 - high) * 2 + (1 - low)
    partners = (across, sibling, far)
    first = me * rows
    local_at = owners * pad
    turn_at = local_at + count
    chunk = most // CHUNKS
    groups = pad // parts
    half = (owners - 1 + 1) // 2
    batches = ((0, half), (half, owners - 1))
    part_rows = pl.ds(pl.multiple_of(part * strip, strip), strip)

    def peer_of(j):
        return lax.rem(me + owners // 2 + ((j + 1) // 2) * (1 - 2 * (j % 2)), owners)

    cl_copy = pltpu.make_async_copy(cl_hbm, cl, in_sem.at[0])
    blocks_copy = pltpu.make_async_copy(blocks_hbm, blocks, in_sem.at[1])
    cl_copy.start()
    blocks_copy.start()

    barrier = pltpu.get_barrier_semaphore()

    @pl.loop(0, owners - 1)
    def _(j):
        pl.semaphore_signal(barrier, inc=1, device_id={"rows": peer_of(j)}, device_id_type=MESH)

    for other in partners:
        pl.semaphore_signal(barrier, inc=1, device_id={"cols": other}, device_id_type=MESH)

    zero_block = jnp.zeros((strip, size), jnp.bfloat16)
    loc[count] = zero_block
    sq[count] = zero_block

    @pl.loop(0, owners)
    def _(o):
        for u in range(band, pad):
            tab[o * pad + u] = zero_block

    cl_copy.wait()
    for k in range(rows):
        for b in range(slots):
            column = cl[b, first + k]
            owner_of[k * slots + b] = jnp.where(column >= 0, jnp.maximum(column, 0) // rows, -1)
    blocks_copy.wait()
    for k in range(rows):
        for b in range(slots):
            n = k * slots + b
            value = blocks[k, b, part_rows, :]
            value = jnp.where(cl[b, first + k] >= 0, value, zero_block)
            loc[n] = value
            tab[local_at + n] = value

    pl.semaphore_wait(barrier, owners - 1 + 3)

    def band_copy(src, dst_owner, peer):
        return pltpu.make_async_remote_copy(
            src_ref=send.at[src],
            dst_ref=tab.at[pl.ds(dst_owner * pad, band)],
            send_sem=send_sem.at[src],
            recv_sem=recv_sem.at[dst_owner],
            device_id={"rows": peer},
            device_id_type=MESH,
        )

    def weight(distance, negative):
        return middle + 1 - distance + jnp.minimum(
            distance - jnp.where(negative, 1, 0), middle - distance
        )

    @pl.loop(0, owners - 1)
    def _(j):
        peer = peer_of(j)
        lowest = jnp.int32(count)
        highest = jnp.int32(-1)
        for n in range(count):
            hit = owner_of[n] == peer
            lowest = jnp.minimum(lowest, jnp.where(hit, n, count))
            highest = jnp.maximum(highest, jnp.where(hit, n, -1))
        has_one = highest >= 0
        has_two = highest > lowest
        code0 = jnp.where(has_one, lowest, 0)
        code1 = jnp.where(has_two, highest, 0)
        row0, row1 = code0 // slots, code1 // slots
        slot0, slot1 = code0 - row0 * slots, code1 - row1 * slots
        away0, away1 = jnp.abs(slot0 - middle), jnp.abs(slot1 - middle)
        weight0 = jnp.where(has_one, weight(away0, slot0 > middle), 0)
        weight1 = jnp.where(has_two, weight(away1, slot1 > middle), 0)
        sign0 = jnp.where(slot0 > middle, -1, 1)
        sign1 = jnp.where(slot1 > middle, -1, 1)
        for u in range(band):
            in0 = u < weight0
            in1 = u < weight0 + weight1
            step = jnp.where(in0, u, u - weight0)
            away = jnp.where(in0, away0, away1)
            sign = jnp.where(in0, sign0, sign1)
            same = step < middle + 1 - away
            move = jnp.where(same, step, -(step - middle + 2 * away))
            entry = jnp.where(in0, row0, row1) * slots + middle + sign * move
            entry = jnp.where(in1, entry, count)
            send[peer, u] = loc[entry]
        band_copy(peer, me, peer).start()
        key0 = cl[slot0, first + row0] * slots + slots - 1 - slot0
        key1 = cl[slot1, first + row1] * slots + slots - 1 - slot1
        swap = has_two & (key1 < key0)
        first_code[peer] = jnp.where(swap, code1, code0)
        first_weight[peer] = jnp.where(
            swap, weight(away1, slot1 < middle), weight(away0, slot0 < middle)
        )

    first_code[me] = 0
    first_weight[me] = 0

    pick = (
        lax.broadcasted_iota(jnp.int32, (strip, size), 1)
        == lax.broadcasted_iota(jnp.int32, (strip, size), 0) + part * strip
    ).astype(jnp.bfloat16)
    for k in range(rows):
        for b in range(slots):
            n = k * slots + b
            block = blocks[k, b]
            block = jnp.where(cl[b, first + k] >= 0, block, jnp.zeros_like(block))
            own[k, :, b * size : (b + 1) * size] = block
            tab[turn_at + local_at + n] = lax.dot_general(
                pick, block, (((1,), (1,)), ((), ())), preferred_element_type=jnp.float32
            ).astype(jnp.bfloat16)

    running = jnp.int32(0)
    for i in range(rows):
        for a in range(slots):
            n = i * slots + a
            column = cl[a, first + i]
            running = running + jnp.where(column >= 0, 1, 0)
            cum[n] = running
            column = jnp.where(column >= 0, column, first + i)
            owner = column // rows
            is_local[n] = jnp.where(owner == me, 1, 0)
            remote_base[n] = owner * pad + jnp.where(first_code[owner] == n, 0, first_weight[owner])
            local_base[n] = local_at + (column - first) * slots

    @pl.loop(0, rows)
    def _(i):
        for a in range(slots):
            for s in range(slots):
                if a == middle or s == middle or abs(a - s) > middle:
                    continue
                away_a, away_s = a - middle, s - middle
                direct = sends(away_s, away_a)
                edge, other = (s, a) if direct else (a, s)
                away_e, away_o = (away_s, away_a) if direct else (away_a, away_s)
                if (away_e > 0) == (away_o > 0):
                    u = abs(away_o) - abs(away_e)
                else:
                    u = middle - abs(away_e) + abs(away_o)
                n = i * slots + edge
                entry = jnp.where(
                    is_local[n] == 1, local_base[n] + (other - edge + middle), remote_base[n] + u
                )
                entries[(i * slots + a) * slots + s] = entry + (0 if direct else turn_at)

    @pl.loop(0, most)
    def _(t):
        entry = jnp.int32(0)
        for n in range(count):
            entry = entry + jnp.where(cum[n] <= t, 1, 0)
        source[t] = entry

    for k in range(rows):
        for a in range(slots):
            lanes = slice(a * size, (a + 1) * size)
            for s in range(slots):
                span = slice(s * strip, (s + 1) * strip)
                if abs(a - s) > middle:
                    win[k, span, lanes] = zero_block
                elif a == middle:
                    win[k, span, lanes] = tab[turn_at + local_at + k * slots + s]
                elif s == middle:
                    win[k, span, lanes] = loc[k * slots + a]

    identity = (
        lax.broadcasted_iota(jnp.int32, (size, size), 0)
        == lax.broadcasted_iota(jnp.int32, (size, size), 1)
    ).astype(jnp.bfloat16)
    wide = parts * size
    line = lax.broadcasted_iota(jnp.int32, (wide, wide), 0)
    from_part, from_block, from_row = line // size, (line % size) // strip, line % strip
    shuffle[...] = (
        lax.broadcasted_iota(jnp.int32, (wide, wide), 1)
        == from_block * size + from_part * strip + from_row
    ).astype(jnp.bfloat16)

    def piece_copy(kind, batch, start):
        begin, end = batches[batch]
        span = pl.ds(begin * groups, (end - begin) * groups)
        other = partners[kind]
        return pltpu.make_async_remote_copy(
            src_ref=turned.at[other, span],
            dst_ref=pieces.at[part if start else other, span],
            send_sem=xsend_sem.at[kind, batch],
            recv_sem=xrecv_sem.at[kind, batch],
            device_id={"cols": other},
            device_id_type=MESH,
        )

    for batch, (begin, end) in enumerate(batches):

        @pl.loop(begin, end)
        def _(j):
            peer = peer_of(j)
            band_copy(peer, peer, peer).wait_recv()
            for g in range(groups):
                stack = jnp.concatenate([tab[peer * pad + g * parts + n] for n in range(parts)], 0)
                flipped = lax.dot_general(
                    identity, stack, (((1,), (1,)), ((), ())), preferred_element_type=jnp.float32
                ).astype(jnp.bfloat16)
                for c in range(parts):
                    turned[c, j * groups + g] = flipped[c * strip : (c + 1) * strip]
                pieces[part, j * groups + g] = turned[part, j * groups + g]

        for kind in range(3):
            piece_copy(kind, batch, True).start()

    for batch, (begin, end) in enumerate(batches):
        for kind in range(3):
            piece_copy(kind, batch, False).wait_recv()

        for c in range(parts):
            lanes = slice(c * size, (c + 1) * size)
            for g in range(begin * groups, end * groups):
                joined[g * strip : (g + 1) * strip, lanes] = pieces[c, g]
        spread = jnp.dot(
            joined[begin * groups * strip : end * groups * strip, :], shuffle[...],
            preferred_element_type=jnp.float32,
        ).astype(jnp.bfloat16)
        for j in range(begin, end):
            at = turn_at + peer_of(j) * pad
            for g in range(groups):
                top = ((j - begin) * groups + g) * strip
                for n in range(parts):
                    tab[at + g * parts + n] = spread[top : top + strip, n * size : (n + 1) * size]

    @pl.loop(0, rows)
    def _(i):
        for a in range(slots):
            for s in range(slots):
                if a == middle or s == middle or abs(a - s) > middle:
                    continue
                win[i, s * strip : (s + 1) * strip, a * size : (a + 1) * size] = tab[
                    entries[(i * slots + a) * slots + s]
                ]
        total = lax.dot_general(
            win[i], own[i], (((1,), (1,)), ((), ())), preferred_element_type=jnp.float32
        )
        for s in range(slots):
            value = total[s * strip : (s + 1) * strip]
            value = jnp.where(cl[s, first + i] >= 0, value, 0.0)
            sq[i * slots + s] = value.astype(jnp.bfloat16)

    def strip_copy(which, piece, peer, sem):
        span = pl.ds(piece * chunk, chunk)
        return pltpu.make_async_remote_copy(
            src_ref=gat.at[which, span],
            dst_ref=gat.at[which, span],
            send_sem=csend_sem.at[sem, piece],
            recv_sem=crecv_sem.at[sem, piece],
            device_id={"cols": peer},
            device_id_type=MESH,
        )

    for piece in range(CHUNKS):
        for t in range(piece * chunk, (piece + 1) * chunk):
            gat[part, t] = sq[source[t]]
        strip_copy(part, piece, across, 0).start()
        strip_copy(part, piece, sibling, 1).start()
    for piece in range(CHUNKS):
        strip_copy(across, piece, across, 0).wait_recv()
        strip_copy(across, piece, sibling, 2).start()
    for piece in range(CHUNKS):
        strip_copy(sibling, piece, sibling, 1).wait_recv()
    for piece in range(CHUNKS):
        strip_copy(far, piece, sibling, 2).wait_recv()

    @pl.loop(0, rows)
    def _(i):
        for a in range(slots):
            n = i * slots + a
            present = cl[a, first + i] >= 0
            entry = jnp.minimum(jnp.maximum(cum[n] - 1, 0), most - 1)
            for c in range(size // strip):
                value = gat[c, entry]
                value = jnp.where(present, value, jnp.zeros_like(value))
                full[a * size + c * strip : a * size + (c + 1) * strip, :] = value
        total = jnp.dot(win[i], full[...], preferred_element_type=jnp.float32)
        for s in range(slots):
            value = 3.0 * sq[i * slots + s].astype(jnp.float32) - 2.0 * total[s * strip : (s + 1) * strip]
            value = jnp.where(cl[s, first + i] >= 0, value, 0.0)
            out[i, s] = value.astype(jnp.bfloat16)

    @pl.loop(0, owners - 1)
    def _(j):
        peer = peer_of(j)
        band_copy(peer, me, peer).wait_send()

    for batch in range(len(batches)):
        for kind in range(3):
            piece_copy(kind, batch, True).wait_send()

    for piece in range(CHUNKS):
        strip_copy(part, piece, across, 0).wait_send()
        strip_copy(part, piece, sibling, 1).wait_send()
        strip_copy(across, piece, sibling, 2).wait_send()


def body(column_lists, block_values):
    rows, slots, size, _ = block_values.shape
    owners = lax.axis_size("rows")
    parts = lax.axis_size("cols")
    assert parts == 4
    strip = size // parts
    middle = (slots - 1) // 2
    band = middle + 1
    pad = -(-band // parts) * parts
    groups = pad // parts
    peers = owners - 1
    count = rows * slots
    most = min(count, rows * rows + CAP * peers)
    most = -(-most // CHUNKS) * CHUNKS
    bf16 = jnp.bfloat16
    table = 2 * (owners * pad + count)
    result = pl.pallas_call(
        functools.partial(kernel, owners, rows, slots, size, strip, band, pad, most),
        out_shape=jax.ShapeDtypeStruct((rows, slots, strip, size), bf16),
        in_specs=[pl.BlockSpec(memory_space=pl.ANY), pl.BlockSpec(memory_space=pl.ANY)],
        out_specs=pl.BlockSpec(memory_space=pltpu.VMEM),
        scratch_shapes=[
            pltpu.SMEM(column_lists.shape[::-1], jnp.int32),
            pltpu.VMEM(block_values.shape, bf16),
            pltpu.VMEM((count + 1, strip, size), bf16),
            pltpu.VMEM((owners, band, strip, size), bf16),
            pltpu.VMEM((table, strip, size), bf16),
            pltpu.VMEM((rows, slots * strip, slots * size), bf16),
            pltpu.VMEM((rows, size, slots * size), bf16),
            pltpu.VMEM((count + 1, strip, size), bf16),
            pltpu.VMEM((parts, most, strip, size), bf16),
            pltpu.VMEM((slots * size, size), bf16),
            pltpu.VMEM((parts, peers * groups, strip, size), bf16),
            pltpu.VMEM((parts, peers * groups, strip, size), bf16),
            pltpu.VMEM((peers * groups * strip, parts * size), bf16),
            pltpu.VMEM((parts * size, parts * size), bf16),
            pltpu.SMEM((count,), jnp.int32),
            pltpu.SMEM((owners,), jnp.int32),
            pltpu.SMEM((owners,), jnp.int32),
            pltpu.SMEM((count,), jnp.int32),
            pltpu.SMEM((count,), jnp.int32),
            pltpu.SMEM((count,), jnp.int32),
            pltpu.SMEM((count * slots,), jnp.int32),
            pltpu.SMEM((count,), jnp.int32),
            pltpu.SMEM((most,), jnp.int32),
            pltpu.SemaphoreType.DMA((owners,)),
            pltpu.SemaphoreType.DMA((owners,)),
            pltpu.SemaphoreType.DMA((3, 2)),
            pltpu.SemaphoreType.DMA((3, 2)),
            pltpu.SemaphoreType.DMA((3, CHUNKS)),
            pltpu.SemaphoreType.DMA((3, CHUNKS)),
            pltpu.SemaphoreType.DMA((2,)),
        ],
        compiler_params=pltpu.CompilerParams(
            collective_id=0, has_side_effects=True, vmem_limit_bytes=52 * 1024 * 1024
        ),
    )(column_lists.T, block_values)
    return jnp.swapaxes(result, 2, 3)


def solution(mesh):
    in_specs = (P(), P("rows", None, None, None))
    out_specs = P("rows", None, None, "cols")
    return jax.shard_map(body, mesh=mesh, in_specs=in_specs, out_specs=out_specs, check_vma=False)
```

```python
import functools

import jax
import jax.numpy as jnp
from jax import lax
from jax.experimental import pallas as pl
from jax.experimental.pallas import tpu as pltpu
from jax.sharding import PartitionSpec as P

CAP = 2
CHUNKS = 2
BATCHES = 3
MESH = pl.DeviceIdType.MESH


def sends(offset, other):
    if (offset > 0) == (other > 0):
        return abs(other) >= abs(offset)
    return abs(other) < abs(offset) or (abs(other) == abs(offset) and offset > 0)


def kernel(
    owners, rows, slots, size, strip, band, pad, most,
    cl_hbm, blocks_hbm, out,
    cl, blocks, loc, send, tab, win, own, sq, gat, full, turned, pieces, joined, shuffle,
    owner_of, first_code, first_weight, remote_base, local_base, is_local, entries, cum, where_sent, source,
    send_sem, recv_sem, xsend_sem, xrecv_sem, csend_sem, crecv_sem, in_sem,
):
    middle = (slots - 1) // 2
    count = rows * slots
    parts = size // strip
    me = lax.axis_index("rows")
    part = lax.axis_index("cols")
    high, low = part // 2, part % 2
    sibling = high * 2 + (1 - low)
    across = (1 - high) * 2 + low
    far = (1 - high) * 2 + (1 - low)
    partners = (across, sibling, far)
    first = me * rows
    local_at = owners * pad
    turn_at = local_at + count
    chunk = (most - rows * rows) // CHUNKS
    groups = pad // parts
    bounds = [-(-(owners - 1) * q // BATCHES) for q in range(BATCHES + 1)]
    batches = list(zip(bounds[:-1], bounds[1:]))
    early = (owners - 1) // 2
    crossing_at = rows * rows
    part_rows = pl.ds(pl.multiple_of(part * strip, strip), strip)

    def peer_of(j):
        return lax.rem(me + owners // 2 + ((j + 1) // 2) * (1 - 2 * (j % 2)), owners)

    cl_copy = pltpu.make_async_copy(cl_hbm, cl, in_sem.at[0])
    blocks_copy = pltpu.make_async_copy(blocks_hbm, blocks, in_sem.at[1])
    cl_copy.start()
    blocks_copy.start()

    barrier = pltpu.get_barrier_semaphore()

    @pl.loop(0, owners - 1)
    def _(j):
        pl.semaphore_signal(barrier, inc=1, device_id={"rows": peer_of(j)}, device_id_type=MESH)

    for other in partners:
        pl.semaphore_signal(barrier, inc=1, device_id={"cols": other}, device_id_type=MESH)

    zero_block = jnp.zeros((strip, size), jnp.bfloat16)
    loc[count] = zero_block
    sq[count] = zero_block

    @pl.loop(0, owners)
    def _(o):
        for u in range(band, pad):
            tab[o * pad + u] = zero_block

    cl_copy.wait()
    for k in range(rows):
        for b in range(slots):
            column = cl[b, first + k]
            owner_of[k * slots + b] = jnp.where(column >= 0, jnp.maximum(column, 0) // rows, -1)
    blocks_copy.wait()
    for k in range(rows):
        for b in range(slots):
            n = k * slots + b
            value = blocks[k, b, part_rows, :]
            value = jnp.where(cl[b, first + k] >= 0, value, zero_block)
            loc[n] = value
            tab[local_at + n] = value

    def band_copy(src, dst_owner, peer):
        return pltpu.make_async_remote_copy(
            src_ref=send.at[src],
            dst_ref=tab.at[pl.ds(dst_owner * pad, band)],
            send_sem=send_sem.at[src],
            recv_sem=recv_sem.at[dst_owner],
            device_id={"rows": peer},
            device_id_type=MESH,
        )

    def weight(distance, negative):
        return middle + 1 - distance + jnp.minimum(
            distance - jnp.where(negative, 1, 0), middle - distance
        )

    def fill(j):
        peer = peer_of(j)
        lowest = jnp.int32(count)
        highest = jnp.int32(-1)
        for n in range(count):
            hit = owner_of[n] == peer
            lowest = jnp.minimum(lowest, jnp.where(hit, n, count))
            highest = jnp.maximum(highest, jnp.where(hit, n, -1))
        has_one = highest >= 0
        has_two = highest > lowest
        code0 = jnp.where(has_one, lowest, 0)
        code1 = jnp.where(has_two, highest, 0)
        row0, row1 = code0 // slots, code1 // slots
        slot0, slot1 = code0 - row0 * slots, code1 - row1 * slots
        away0, away1 = jnp.abs(slot0 - middle), jnp.abs(slot1 - middle)
        weight0 = jnp.where(has_one, weight(away0, slot0 > middle), 0)
        weight1 = jnp.where(has_two, weight(away1, slot1 > middle), 0)
        sign0 = jnp.where(slot0 > middle, -1, 1)
        sign1 = jnp.where(slot1 > middle, -1, 1)
        for u in range(band):
            in0 = u < weight0
            in1 = u < weight0 + weight1
            step = jnp.where(in0, u, u - weight0)
            away = jnp.where(in0, away0, away1)
            sign = jnp.where(in0, sign0, sign1)
            same = step < middle + 1 - away
            move = jnp.where(same, step, -(step - middle + 2 * away))
            entry = jnp.where(in0, row0, row1) * slots + middle + sign * move
            entry = jnp.where(in1, entry, count)
            send[peer, u] = loc[entry]
        key0 = cl[slot0, first + row0] * slots + slots - 1 - slot0
        key1 = cl[slot1, first + row1] * slots + slots - 1 - slot1
        swap = has_two & (key1 < key0)
        first_code[peer] = jnp.where(swap, code1, code0)
        first_weight[peer] = jnp.where(
            swap, weight(away1, slot1 < middle), weight(away0, slot0 < middle)
        )

    @pl.loop(0, early)
    def _(j):
        fill(j)

    pl.semaphore_wait(barrier, owners - 1 + 3)

    @pl.loop(0, early)
    def _(j):
        band_copy(peer_of(j), me, peer_of(j)).start()

    @pl.loop(early, owners - 1)
    def _(j):
        fill(j)
        band_copy(peer_of(j), me, peer_of(j)).start()

    first_code[me] = 0
    first_weight[me] = 0

    pick = (
        lax.broadcasted_iota(jnp.int32, (strip, size), 1)
        == lax.broadcasted_iota(jnp.int32, (strip, size), 0) + part * strip
    ).astype(jnp.bfloat16)
    for k in range(rows):
        for b in range(slots):
            n = k * slots + b
            block = blocks[k, b]
            block = jnp.where(cl[b, first + k] >= 0, block, jnp.zeros_like(block))
            own[k, :, b * size : (b + 1) * size] = block
            tab[turn_at + local_at + n] = lax.dot_general(
                pick, block, (((1,), (1,)), ((), ())), preferred_element_type=jnp.float32
            ).astype(jnp.bfloat16)

    running = jnp.int32(0)
    for i in range(rows):
        for a in range(slots):
            n = i * slots + a
            column = cl[a, first + i]
            absent = column < 0
            column = jnp.where(absent, first + i, column)
            owner = column // rows
            running = running + jnp.where(owner == me, 0, 1)
            cum[n] = running
            where_sent[n] = jnp.where(
                owner == me,
                i * rows + column - first,
                jnp.minimum(crossing_at + running - 1, most - 1),
            )
            is_local[n] = jnp.where(owner == me, 1, 0)
            remote_base[n] = owner * pad + jnp.where(first_code[owner] == n, 0, first_weight[owner])
            local_base[n] = local_at + (column - first) * slots

    @pl.loop(0, rows)
    def _(i):
        for a in range(slots):
            for s in range(slots):
                if a == middle or s == middle or abs(a - s) > middle:
                    continue
                away_a, away_s = a - middle, s - middle
                direct = sends(away_s, away_a)
                edge, other = (s, a) if direct else (a, s)
                away_e, away_o = (away_s, away_a) if direct else (away_a, away_s)
                if (away_e > 0) == (away_o > 0):
                    u = abs(away_o) - abs(away_e)
                else:
                    u = middle - abs(away_e) + abs(away_o)
                n = i * slots + edge
                entry = jnp.where(
                    is_local[n] == 1, local_base[n] + (other - edge + middle), remote_base[n] + u
                )
                entries[(i * slots + a) * slots + s] = entry + (0 if direct else turn_at)

    for k in range(rows):
        for a in range(slots):
            lanes = slice(a * size, (a + 1) * size)
            for s in range(slots):
                span = slice(s * strip, (s + 1) * strip)
                if abs(a - s) > middle:
                    win[k, span, lanes] = zero_block
                elif a == middle:
                    win[k, span, lanes] = tab[turn_at + local_at + k * slots + s]
                elif s == middle:
                    win[k, span, lanes] = loc[k * slots + a]

    identity = (
        lax.broadcasted_iota(jnp.int32, (size, size), 0)
        == lax.broadcasted_iota(jnp.int32, (size, size), 1)
    ).astype(jnp.bfloat16)
    wide = parts * size
    line = lax.broadcasted_iota(jnp.int32, (wide, wide), 0)
    from_part, from_block, from_row = line // size, (line % size) // strip, line % strip
    shuffle[...] = (
        lax.broadcasted_iota(jnp.int32, (wide, wide), 1)
        == from_block * size + from_part * strip + from_row
    ).astype(jnp.bfloat16)

    def piece_copy(kind, batch, start):
        begin, end = batches[batch]
        span = pl.ds(begin * groups, (end - begin) * groups)
        other = partners[kind]
        return pltpu.make_async_remote_copy(
            src_ref=turned.at[other, span],
            dst_ref=pieces.at[part if start else other, span],
            send_sem=xsend_sem.at[kind, batch],
            recv_sem=xrecv_sem.at[kind, batch],
            device_id={"cols": other},
            device_id_type=MESH,
        )

    for batch, (begin, end) in enumerate(batches):

        @pl.loop(begin, end)
        def _(j):
            peer = peer_of(j)
            band_copy(peer, peer, peer).wait_recv()
            for g in range(groups):
                stack = jnp.concatenate([tab[peer * pad + g * parts + n] for n in range(parts)], 0)
                flipped = lax.dot_general(
                    identity, stack, (((1,), (1,)), ((), ())), preferred_element_type=jnp.float32
                ).astype(jnp.bfloat16)
                for c in range(parts):
                    turned[c, j * groups + g] = flipped[c * strip : (c + 1) * strip]
                pieces[part, j * groups + g] = turned[part, j * groups + g]

        for kind in range(3):
            piece_copy(kind, batch, True).start()

        if batch == 0:
            for i in range(rows):
                for k in range(rows):
                    entry = jnp.int32(count)
                    for a in range(slots):
                        entry = jnp.where(cl[a, first + i] == first + k, i * slots + a, entry)
                    source[i * rows + k] = entry

            @pl.loop(0, most - crossing_at)
            def _(t):
                entry = jnp.int32(0)
                for n in range(count):
                    entry = entry + jnp.where(cum[n] <= t, 1, 0)
                source[crossing_at + t] = entry

    for batch, (begin, end) in enumerate(batches):
        for kind in range(3):
            piece_copy(kind, batch, False).wait_recv()

        for c in range(parts):
            lanes = slice(c * size, (c + 1) * size)
            for g in range(begin * groups, end * groups):
                joined[g * strip : (g + 1) * strip, lanes] = pieces[c, g]
        spread = jnp.dot(
            joined[begin * groups * strip : end * groups * strip, :], shuffle[...],
            preferred_element_type=jnp.float32,
        ).astype(jnp.bfloat16)
        for j in range(begin, end):
            at = turn_at + peer_of(j) * pad
            for g in range(groups):
                top = ((j - begin) * groups + g) * strip
                for n in range(parts):
                    tab[at + g * parts + n] = spread[top : top + strip, n * size : (n + 1) * size]

    spans = [(i * rows, rows) for i in range(rows)]
    spans += [(crossing_at + q * chunk, chunk) for q in range(CHUNKS)]

    def strip_copy(which, piece, peer, sem):
        span = pl.ds(*spans[piece])
        return pltpu.make_async_remote_copy(
            src_ref=gat.at[which, span],
            dst_ref=gat.at[which, span],
            send_sem=csend_sem.at[sem, piece],
            recv_sem=crecv_sem.at[sem, piece],
            device_id={"cols": peer},
            device_id_type=MESH,
        )

    def send_strips(piece):
        begin, length = spans[piece]
        for t in range(begin, begin + length):
            gat[part, t] = sq[source[t]]
        strip_copy(part, piece, across, 0).start()
        strip_copy(part, piece, sibling, 1).start()

    def build(i):
        for a in range(slots):
            for s in range(slots):
                if a == middle or s == middle or abs(a - s) > middle:
                    continue
                win[i, s * strip : (s + 1) * strip, a * size : (a + 1) * size] = tab[
                    entries[(i * slots + a) * slots + s]
                ]

    build(0)
    for i in range(rows):
        if i + 1 < rows:
            build(i + 1)
        total = lax.dot_general(
            win[i], own[i], (((1,), (1,)), ((), ())), preferred_element_type=jnp.float32
        )
        for s in range(slots):
            value = total[s * strip : (s + 1) * strip]
            value = jnp.where(cl[s, first + i] >= 0, value, 0.0)
            sq[i * slots + s] = value.astype(jnp.bfloat16)
        send_strips(i)
    for piece in range(rows, len(spans)):
        send_strips(piece)

    for piece in range(len(spans)):
        strip_copy(across, piece, across, 0).wait_recv()
        strip_copy(across, piece, sibling, 2).start()
    for piece in range(len(spans)):
        strip_copy(sibling, piece, sibling, 1).wait_recv()
    for piece in range(len(spans)):
        strip_copy(far, piece, sibling, 2).wait_recv()

    for i in range(rows):
        for a in range(slots):
            n = i * slots + a
            present = cl[a, first + i] >= 0
            entry = where_sent[n]
            for c in range(parts):
                value = gat[c, entry]
                value = jnp.where(present, value, zero_block)
                full[i, a * size + c * strip : a * size + (c + 1) * strip, :] = value
        total = jnp.dot(win[i], full[i], preferred_element_type=jnp.float32)
        for s in range(slots):
            value = 3.0 * sq[i * slots + s].astype(jnp.float32) - 2.0 * total[s * strip : (s + 1) * strip]
            value = jnp.where(cl[s, first + i] >= 0, value, 0.0)
            out[i, s] = value.astype(jnp.bfloat16)

    @pl.loop(0, owners - 1)
    def _(j):
        peer = peer_of(j)
        band_copy(peer, me, peer).wait_send()

    for batch in range(len(batches)):
        for kind in range(3):
            piece_copy(kind, batch, True).wait_send()

    for piece in range(len(spans)):
        strip_copy(part, piece, across, 0).wait_send()
        strip_copy(part, piece, sibling, 1).wait_send()
        strip_copy(across, piece, sibling, 2).wait_send()


def body(column_lists, block_values):
    rows, slots, size, _ = block_values.shape
    owners = lax.axis_size("rows")
    parts = lax.axis_size("cols")
    assert parts == 4
    strip = size // parts
    middle = (slots - 1) // 2
    band = middle + 1
    pad = -(-band // parts) * parts
    groups = pad // parts
    peers = owners - 1
    count = rows * slots
    crossing = min(count - rows, CAP * peers)
    most = rows * rows + -(-crossing // CHUNKS) * CHUNKS
    bf16 = jnp.bfloat16
    table = 2 * (owners * pad + count)
    result = pl.pallas_call(
        functools.partial(kernel, owners, rows, slots, size, strip, band, pad, most),
        out_shape=jax.ShapeDtypeStruct((rows, slots, strip, size), bf16),
        in_specs=[pl.BlockSpec(memory_space=pl.ANY), pl.BlockSpec(memory_space=pl.ANY)],
        out_specs=pl.BlockSpec(memory_space=pltpu.VMEM),
        scratch_shapes=[
            pltpu.SMEM(column_lists.shape[::-1], jnp.int32),
            pltpu.VMEM(block_values.shape, bf16),
            pltpu.VMEM((count + 1, strip, size), bf16),
            pltpu.VMEM((owners, band, strip, size), bf16),
            pltpu.VMEM((table, strip, size), bf16),
            pltpu.VMEM((rows, slots * strip, slots * size), bf16),
            pltpu.VMEM((rows, size, slots * size), bf16),
            pltpu.VMEM((count + 1, strip, size), bf16),
            pltpu.VMEM((parts, most, strip, size), bf16),
            pltpu.VMEM((rows, slots * size, size), bf16),
            pltpu.VMEM((parts, peers * groups, strip, size), bf16),
            pltpu.VMEM((parts, peers * groups, strip, size), bf16),
            pltpu.VMEM((peers * groups * strip, parts * size), bf16),
            pltpu.VMEM((parts * size, parts * size), bf16),
            pltpu.SMEM((count,), jnp.int32),
            pltpu.SMEM((owners,), jnp.int32),
            pltpu.SMEM((owners,), jnp.int32),
            pltpu.SMEM((count,), jnp.int32),
            pltpu.SMEM((count,), jnp.int32),
            pltpu.SMEM((count,), jnp.int32),
            pltpu.SMEM((count * slots,), jnp.int32),
            pltpu.SMEM((count,), jnp.int32),
            pltpu.SMEM((count,), jnp.int32),
            pltpu.SMEM((most,), jnp.int32),
            pltpu.SemaphoreType.DMA((owners,)),
            pltpu.SemaphoreType.DMA((owners,)),
            pltpu.SemaphoreType.DMA((3, BATCHES)),
            pltpu.SemaphoreType.DMA((3, BATCHES)),
            pltpu.SemaphoreType.DMA((3, rows + CHUNKS)),
            pltpu.SemaphoreType.DMA((3, rows + CHUNKS)),
            pltpu.SemaphoreType.DMA((2,)),
        ],
        compiler_params=pltpu.CompilerParams(
            collective_id=0, has_side_effects=True, vmem_limit_bytes=52 * 1024 * 1024
        ),
    )(column_lists.T, block_values)
    return jnp.swapaxes(result, 2, 3)


def solution(mesh):
    in_specs = (P(), P("rows", None, None, None))
    out_specs = P("rows", None, None, "cols")
    return jax.shard_map(body, mesh=mesh, in_specs=in_specs, out_specs=out_specs, check_vma=False)
```

```python
import functools

import jax
import jax.numpy as jnp
from jax import lax
from jax.experimental import pallas as pl
from jax.experimental.pallas import tpu as pltpu
from jax.sharding import PartitionSpec as P

CAP = 2
CHUNKS = 2
BATCHES = 3
MESH = pl.DeviceIdType.MESH


def sends(offset, other):
    if (offset > 0) == (other > 0):
        return abs(other) >= abs(offset)
    return abs(other) < abs(offset) or (abs(other) == abs(offset) and offset > 0)


def kernel(
    owners, rows, slots, size, strip, band, pad, most,
    cl_hbm, blocks_hbm, out,
    cl, blocks, loc, send, tab, win, own, sq, gat, full, turned, pieces, joined, shuffle,
    owner_of, first_code, first_weight, remote_base, local_base, is_local, entries, cum, where_sent, source,
    send_sem, recv_sem, xsend_sem, xrecv_sem, csend_sem, crecv_sem, in_sem,
):
    middle = (slots - 1) // 2
    count = rows * slots
    parts = size // strip
    me = lax.axis_index("rows")
    part = lax.axis_index("cols")
    high, low = part // 2, part % 2
    sibling = high * 2 + (1 - low)
    across = (1 - high) * 2 + low
    far = (1 - high) * 2 + (1 - low)
    partners = (across, sibling, far)
    first = me * rows
    local_at = owners * pad
    turn_at = local_at + count
    chunk = (most - rows * rows) // CHUNKS
    groups = pad // parts
    bounds = [0, owners // 2 - 1, (3 * owners) // 4 - 1, owners - 1]
    batches = list(zip(bounds[:-1], bounds[1:]))
    early = (owners - 1) // 2
    crossing_at = rows * rows
    part_rows = pl.ds(pl.multiple_of(part * strip, strip), strip)

    def peer_of(j):
        peer, bit = 0, 1
        while bit < owners:
            peer = peer + ((me // bit + (j + 1) // bit) % 2) * bit
            bit *= 2
        return peer

    def in_turn(j):
        return (j // 2 + owners // 2) * (1 - j % 2) + ((j + 1) // 2) * (j % 2) - 1

    cl_copy = pltpu.make_async_copy(cl_hbm, cl, in_sem.at[0])
    loc_copy = pltpu.make_async_copy(blocks_hbm.at[:, :, part_rows, :], loc, in_sem.at[2])
    blocks_copy = pltpu.make_async_copy(blocks_hbm, blocks, in_sem.at[1])
    cl_copy.start()
    loc_copy.start()
    blocks_copy.start()

    barrier = pltpu.get_barrier_semaphore()

    @pl.loop(0, owners - 1)
    def _(j):
        pl.semaphore_signal(barrier, inc=1, device_id={"rows": peer_of(j)}, device_id_type=MESH)

    for other in partners:
        pl.semaphore_signal(barrier, inc=1, device_id={"cols": other}, device_id_type=MESH)

    zero_block = jnp.zeros((strip, size), jnp.bfloat16)
    sq[count] = zero_block

    @pl.loop(0, owners)
    def _(o):
        for u in range(band, pad):
            tab[o * pad + u] = zero_block

    cl_copy.wait()
    for k in range(rows):
        for b in range(slots):
            column = cl[b, first + k]
            owner_of[k * slots + b] = jnp.where(column >= 0, jnp.maximum(column, 0) // rows, -1)
    loc_copy.wait()

    def band_copy(src, dst_owner, peer):
        return pltpu.make_async_remote_copy(
            src_ref=send.at[src],
            dst_ref=tab.at[pl.ds(dst_owner * pad, band)],
            send_sem=send_sem.at[src],
            recv_sem=recv_sem.at[dst_owner],
            device_id={"rows": peer},
            device_id_type=MESH,
        )

    def weight(distance, negative):
        return middle + 1 - distance + jnp.minimum(
            distance - jnp.where(negative, 1, 0), middle - distance
        )

    def fill(peer):
        lowest = jnp.int32(count)
        highest = jnp.int32(-1)
        for n in range(count):
            hit = owner_of[n] == peer
            lowest = jnp.minimum(lowest, jnp.where(hit, n, count))
            highest = jnp.maximum(highest, jnp.where(hit, n, -1))
        has_one = highest >= 0
        has_two = highest > lowest
        code0 = jnp.where(has_one, lowest, 0)
        code1 = jnp.where(has_two, highest, 0)
        row0, row1 = code0 // slots, code1 // slots
        slot0, slot1 = code0 - row0 * slots, code1 - row1 * slots
        away0, away1 = jnp.abs(slot0 - middle), jnp.abs(slot1 - middle)
        weight0 = jnp.where(has_one, weight(away0, slot0 > middle), 0)
        weight1 = jnp.where(has_two, weight(away1, slot1 > middle), 0)
        sign0 = jnp.where(slot0 > middle, -1, 1)
        sign1 = jnp.where(slot1 > middle, -1, 1)
        for u in range(band):
            in0 = u < weight0
            in1 = u < weight0 + weight1
            step = jnp.where(in0, u, u - weight0)
            away = jnp.where(in0, away0, away1)
            sign = jnp.where(in0, sign0, sign1)
            same = step < middle + 1 - away
            move = jnp.where(same, step, -(step - middle + 2 * away))
            row = jnp.where(in0, row0, row1)
            slot = jnp.where(in1, middle + sign * move, middle)
            used = in1 & (owner_of[row * slots + slot] >= 0)
            send[peer, u] = jnp.where(used, loc[row, slot], zero_block)
        key0 = cl[slot0, first + row0] * slots + slots - 1 - slot0
        key1 = cl[slot1, first + row1] * slots + slots - 1 - slot1
        swap = has_two & (key1 < key0)
        first_code[peer] = jnp.where(swap, code1, code0)
        first_weight[peer] = jnp.where(
            swap, weight(away1, slot1 < middle), weight(away0, slot0 < middle)
        )

    @pl.loop(0, early)
    def _(j):
        fill(peer_of(in_turn(j)))

    pl.semaphore_wait(barrier, owners - 1 + 3)

    @pl.loop(0, early)
    def _(j):
        peer = peer_of(in_turn(j))
        band_copy(peer, me, peer).start()

    @pl.loop(early, owners - 1)
    def _(j):
        peer = peer_of(in_turn(j))
        fill(peer)
        band_copy(peer, me, peer).start()

    first_code[me] = 0
    first_weight[me] = 0

    blocks_copy.wait()

    @pl.loop(0, rows)
    def _(k):
        for b in range(slots):
            n = k * slots + b
            present = cl[b, first + k] >= 0
            block = blocks[k, b]
            block = jnp.where(present, block, jnp.zeros_like(block))
            own[k, b * size : (b + 1) * size, :] = block.T
            value = jnp.where(present, loc[k, b], zero_block)
            tab[local_at + n] = value
            if b != middle:
                win[k, middle * strip : (middle + 1) * strip, b * size : (b + 1) * size] = value
        for b in range(slots):
            value = own[k, pl.ds(pl.multiple_of(b * size + part * strip, strip), strip), :]
            tab[turn_at + local_at + k * slots + b] = value
            win[k, b * strip : (b + 1) * strip, middle * size : (middle + 1) * size] = value

    running = jnp.int32(0)
    for i in range(rows):
        for a in range(slots):
            n = i * slots + a
            column = cl[a, first + i]
            absent = column < 0
            column = jnp.where(absent, first + i, column)
            owner = column // rows
            running = running + jnp.where(owner == me, 0, 1)
            cum[n] = running
            where_sent[n] = jnp.where(
                owner == me,
                i * rows + column - first,
                jnp.minimum(crossing_at + running - 1, most - 1),
            )
            is_local[n] = jnp.where(owner == me, 1, 0)
            remote_base[n] = owner * pad + jnp.where(first_code[owner] == n, 0, first_weight[owner])
            local_base[n] = local_at + (column - first) * slots

    @pl.loop(0, rows)
    def _(i):
        for a in range(slots):
            for s in range(slots):
                if a == middle or s == middle or abs(a - s) > middle:
                    continue
                away_a, away_s = a - middle, s - middle
                direct = sends(away_s, away_a)
                edge, other = (s, a) if direct else (a, s)
                away_e, away_o = (away_s, away_a) if direct else (away_a, away_s)
                if (away_e > 0) == (away_o > 0):
                    u = abs(away_o) - abs(away_e)
                else:
                    u = middle - abs(away_e) + abs(away_o)
                n = i * slots + edge
                entry = jnp.where(
                    is_local[n] == 1, local_base[n] + (other - edge + middle), remote_base[n] + u
                )
                entries[(i * slots + a) * slots + s] = entry + (0 if direct else turn_at)

    @pl.loop(0, rows)
    def _(k):
        for a in range(slots):
            for s in range(slots):
                if abs(a - s) > middle:
                    win[k, s * strip : (s + 1) * strip, a * size : (a + 1) * size] = zero_block

    wide = parts * size
    line = lax.broadcasted_iota(jnp.int32, (wide, wide), 0)
    from_part, from_block, from_row = line // size, (line % size) // strip, line % strip
    shuffle[...] = (
        lax.broadcasted_iota(jnp.int32, (wide, wide), 1)
        == from_block * size + from_part * strip + from_row
    ).astype(jnp.bfloat16)

    def piece_copy(kind, batch, start):
        begin, end = batches[batch]
        span = pl.ds(begin * groups, (end - begin) * groups)
        other = partners[kind]
        return pltpu.make_async_remote_copy(
            src_ref=turned.at[other, span],
            dst_ref=pieces.at[part if start else other, span],
            send_sem=xsend_sem.at[kind, batch],
            recv_sem=xrecv_sem.at[kind, batch],
            device_id={"cols": other},
            device_id_type=MESH,
        )

    for batch, (begin, end) in enumerate(batches):

        @pl.loop(begin, end)
        def _(j):
            peer = peer_of(j)
            band_copy(peer, peer, peer).wait_recv()

        @pl.loop(begin, end, unroll=min(end - begin, 4))
        def _(j):
            peer = peer_of(j)
            for g in range(groups):
                stack = jnp.concatenate([tab[peer * pad + g * parts + n] for n in range(parts)], 0)
                flipped = stack.T
                for c in range(parts):
                    turned[c, j * groups + g] = flipped[c * strip : (c + 1) * strip]
                pieces[part, j * groups + g] = turned[part, j * groups + g]

        for kind in range(3):
            piece_copy(kind, batch, True).start()

        if batch == 0:
            for i in range(rows):
                for k in range(rows):
                    entry = jnp.int32(count)
                    for a in range(slots):
                        entry = jnp.where(cl[a, first + i] == first + k, i * slots + a, entry)
                    source[i * rows + k] = entry

            @pl.loop(0, most - crossing_at)
            def _(t):
                entry = jnp.int32(0)
                for n in range(count):
                    entry = entry + jnp.where(cum[n] <= t, 1, 0)
                source[crossing_at + t] = entry

    for batch, (begin, end) in enumerate(batches):
        for kind in range(3):
            piece_copy(kind, batch, False).wait_recv()

        for c in range(parts):
            lanes = slice(c * size, (c + 1) * size)
            for g in range(begin * groups, end * groups):
                joined[g * strip : (g + 1) * strip, lanes] = pieces[c, g]
        spread = jnp.dot(
            joined[begin * groups * strip : end * groups * strip, :], shuffle[...],
            preferred_element_type=jnp.float32,
        ).astype(jnp.bfloat16)
        for j in range(begin, end):
            at = turn_at + peer_of(j) * pad
            for g in range(groups):
                top = ((j - begin) * groups + g) * strip
                for n in range(parts):
                    tab[at + g * parts + n] = spread[top : top + strip, n * size : (n + 1) * size]

    spans = [(i * rows, rows) for i in range(rows)]
    spans += [(crossing_at + q * chunk, chunk) for q in range(CHUNKS)]

    def strip_copy(which, piece, peer, sem):
        span = pl.ds(*spans[piece])
        return pltpu.make_async_remote_copy(
            src_ref=gat.at[which, span],
            dst_ref=gat.at[which, span],
            send_sem=csend_sem.at[sem, piece],
            recv_sem=crecv_sem.at[sem, piece],
            device_id={"cols": peer},
            device_id_type=MESH,
        )

    def send_strips(piece):
        begin, length = spans[piece]
        for t in range(begin, begin + length):
            gat[part, t] = sq[source[t]]
        strip_copy(part, piece, across, 0).start()
        strip_copy(part, piece, sibling, 1).start()

    def build(i):
        for a in range(slots):
            for s in range(slots):
                if a == middle or s == middle or abs(a - s) > middle:
                    continue
                win[i, s * strip : (s + 1) * strip, a * size : (a + 1) * size] = tab[
                    entries[(i * slots + a) * slots + s]
                ]

    build(0)
    for i in range(rows):
        if i + 1 < rows:
            build(i + 1)
        total = jnp.dot(win[i], own[i], preferred_element_type=jnp.float32)
        for s in range(slots):
            value = total[s * strip : (s + 1) * strip]
            value = jnp.where(cl[s, first + i] >= 0, value, 0.0)
            sq[i * slots + s] = value.astype(jnp.bfloat16)
        send_strips(i)
    for piece in range(rows, len(spans)):
        send_strips(piece)

    for piece in range(len(spans)):
        strip_copy(across, piece, across, 0).wait_recv()
        strip_copy(across, piece, sibling, 2).start()
    for piece in range(len(spans)):
        strip_copy(sibling, piece, sibling, 1).wait_recv()
    for piece in range(len(spans)):
        strip_copy(far, piece, sibling, 2).wait_recv()

    for i in range(rows):
        for a in range(slots):
            n = i * slots + a
            present = cl[a, first + i] >= 0
            entry = where_sent[n]
            for c in range(parts):
                value = gat[c, entry]
                value = jnp.where(present, value, zero_block)
                full[i, a * size + c * strip : a * size + (c + 1) * strip, :] = value
        total = jnp.dot(win[i], full[i], preferred_element_type=jnp.float32)
        for s in range(slots):
            value = 3.0 * sq[i * slots + s].astype(jnp.float32) - 2.0 * total[s * strip : (s + 1) * strip]
            value = jnp.where(cl[s, first + i] >= 0, value, 0.0)
            out[i, s] = value.astype(jnp.bfloat16)

    @pl.loop(0, owners - 1)
    def _(j):
        peer = peer_of(j)
        band_copy(peer, me, peer).wait_send()

    for batch in range(len(batches)):
        for kind in range(3):
            piece_copy(kind, batch, True).wait_send()

    for piece in range(len(spans)):
        strip_copy(part, piece, across, 0).wait_send()
        strip_copy(part, piece, sibling, 1).wait_send()
        strip_copy(across, piece, sibling, 2).wait_send()


def body(column_lists, block_values):
    rows, slots, size, _ = block_values.shape
    owners = lax.axis_size("rows")
    parts = lax.axis_size("cols")
    assert parts == 4
    strip = size // parts
    middle = (slots - 1) // 2
    band = middle + 1
    pad = -(-band // parts) * parts
    groups = pad // parts
    peers = owners - 1
    count = rows * slots
    crossing = min(count - rows, CAP * peers)
    most = rows * rows + -(-crossing // CHUNKS) * CHUNKS
    bf16 = jnp.bfloat16
    table = 2 * (owners * pad + count)
    result = pl.pallas_call(
        functools.partial(kernel, owners, rows, slots, size, strip, band, pad, most),
        out_shape=jax.ShapeDtypeStruct((rows, slots, strip, size), bf16),
        in_specs=[pl.BlockSpec(memory_space=pl.ANY), pl.BlockSpec(memory_space=pl.ANY)],
        out_specs=pl.BlockSpec(memory_space=pltpu.VMEM),
        scratch_shapes=[
            pltpu.SMEM(column_lists.shape[::-1], jnp.int32),
            pltpu.VMEM(block_values.shape, bf16),
            pltpu.VMEM((rows, slots, strip, size), bf16),
            pltpu.VMEM((owners, band, strip, size), bf16),
            pltpu.VMEM((table, strip, size), bf16),
            pltpu.VMEM((rows, slots * strip, slots * size), bf16),
            pltpu.VMEM((rows, slots * size, size), bf16),
            pltpu.VMEM((count + 1, strip, size), bf16),
            pltpu.VMEM((parts, most, strip, size), bf16),
            pltpu.VMEM((rows, slots * size, size), bf16),
            pltpu.VMEM((parts, peers * groups, strip, size), bf16),
            pltpu.VMEM((parts, peers * groups, strip, size), bf16),
            pltpu.VMEM((peers * groups * strip, parts * size), bf16),
            pltpu.VMEM((parts * size, parts * size), bf16),
            pltpu.SMEM((count,), jnp.int32),
            pltpu.SMEM((owners,), jnp.int32),
            pltpu.SMEM((owners,), jnp.int32),
            pltpu.SMEM((count,), jnp.int32),
            pltpu.SMEM((count,), jnp.int32),
            pltpu.SMEM((count,), jnp.int32),
            pltpu.SMEM((count * slots,), jnp.int32),
            pltpu.SMEM((count,), jnp.int32),
            pltpu.SMEM((count,), jnp.int32),
            pltpu.SMEM((most,), jnp.int32),
            pltpu.SemaphoreType.DMA((owners,)),
            pltpu.SemaphoreType.DMA((owners,)),
            pltpu.SemaphoreType.DMA((3, BATCHES)),
            pltpu.SemaphoreType.DMA((3, BATCHES)),
            pltpu.SemaphoreType.DMA((3, rows + CHUNKS)),
            pltpu.SemaphoreType.DMA((3, rows + CHUNKS)),
            pltpu.SemaphoreType.DMA((3,)),
        ],
        compiler_params=pltpu.CompilerParams(
            collective_id=0, has_side_effects=True, vmem_limit_bytes=52 * 1024 * 1024
        ),
    )(column_lists.T, block_values)
    return jnp.swapaxes(result, 2, 3)


def solution(mesh):
    in_specs = (P(), P("rows", None, None, None))
    out_specs = P("rows", None, None, "cols")
    return jax.shard_map(body, mesh=mesh, in_specs=in_specs, out_specs=out_specs, check_vma=False)
```

```python
import functools

import jax
import jax.numpy as jnp
from jax import lax
from jax.experimental import pallas as pl
from jax.experimental.pallas import tpu as pltpu
from jax.sharding import PartitionSpec as P

CAP = 2
CHUNKS = 2
BATCHES = 3
MESH = pl.DeviceIdType.MESH


def sends(offset, other):
    if (offset > 0) == (other > 0):
        return abs(other) >= abs(offset)
    return abs(other) < abs(offset) or (abs(other) == abs(offset) and offset > 0)


def kernel(
    owners, rows, slots, size, strip, band, pad, most,
    cl_hbm, blocks_hbm, out,
    cl, blocks, loc, send, tab, win, own, sq, near, away, full, halves, partial, turned, pieces, joined, shuffle,
    owner_of, first_code, first_weight, remote_base, local_base, is_local, entries, cum, where_sent, source,
    send_sem, recv_sem, xsend_sem, xrecv_sem, csend_sem, crecv_sem, in_sem,
):
    middle = (slots - 1) // 2
    count = rows * slots
    parts = size // strip
    me = lax.axis_index("rows")
    part = lax.axis_index("cols")
    high, low = part // 2, part % 2
    sibling = high * 2 + (1 - low)
    across = (1 - high) * 2 + low
    far = (1 - high) * 2 + (1 - low)
    partners = (across, far, sibling)
    first = me * rows
    local_at = owners * pad
    turn_at = local_at + count
    chunk = (most - rows * rows) // CHUNKS
    groups = pad // parts
    bounds = [0, owners // 2 - 1, (3 * owners) // 4 - 1, owners - 1]
    batches = list(zip(bounds[:-1], bounds[1:]))
    early = 1
    crossing_at = rows * rows
    part_rows = pl.ds(pl.multiple_of(part * strip, strip), strip)

    def peer_of(j):
        peer, bit = 0, 1
        while bit < owners:
            peer = peer + ((me // bit + (j + 1) // bit) % 2) * bit
            bit *= 2
        return peer

    def in_turn(j):
        return (j // 2 + owners // 2) * (1 - j % 2) + ((j + 1) // 2) * (j % 2) - 1

    cl_copy = pltpu.make_async_copy(cl_hbm, cl, in_sem.at[0])
    loc_copy = pltpu.make_async_copy(blocks_hbm.at[:, :, part_rows, :], loc, in_sem.at[2])
    blocks_copy = pltpu.make_async_copy(blocks_hbm, blocks, in_sem.at[1])
    cl_copy.start()
    loc_copy.start()
    blocks_copy.start()

    barrier = pltpu.get_barrier_semaphore()

    @pl.loop(0, owners - 1)
    def _(j):
        pl.semaphore_signal(barrier, inc=1, device_id={"rows": peer_of(j)}, device_id_type=MESH)

    for other in partners:
        pl.semaphore_signal(barrier, inc=1, device_id={"cols": other}, device_id_type=MESH)

    zero_block = jnp.zeros((strip, size), jnp.bfloat16)
    sq[count] = zero_block

    @pl.loop(0, owners)
    def _(o):
        for u in range(band, pad):
            tab[o * pad + u] = zero_block

    cl_copy.wait()
    for k in range(rows):
        for b in range(slots):
            column = cl[b, first + k]
            owner_of[k * slots + b] = jnp.where(column >= 0, jnp.maximum(column, 0) // rows, -1)
    loc_copy.wait()

    def band_copy(src, dst_owner, peer):
        return pltpu.make_async_remote_copy(
            src_ref=send.at[src],
            dst_ref=tab.at[pl.ds(dst_owner * pad, band)],
            send_sem=send_sem.at[src],
            recv_sem=recv_sem.at[dst_owner],
            device_id={"rows": peer},
            device_id_type=MESH,
        )

    def weight(distance, negative):
        return middle + 1 - distance + jnp.minimum(
            distance - jnp.where(negative, 1, 0), middle - distance
        )

    def fill(peer):
        lowest = jnp.int32(count)
        highest = jnp.int32(-1)
        for n in range(count):
            hit = owner_of[n] == peer
            lowest = jnp.minimum(lowest, jnp.where(hit, n, count))
            highest = jnp.maximum(highest, jnp.where(hit, n, -1))
        has_one = highest >= 0
        has_two = highest > lowest
        code0 = jnp.where(has_one, lowest, 0)
        code1 = jnp.where(has_two, highest, 0)
        row0, row1 = code0 // slots, code1 // slots
        slot0, slot1 = code0 - row0 * slots, code1 - row1 * slots
        away0, away1 = jnp.abs(slot0 - middle), jnp.abs(slot1 - middle)
        weight0 = jnp.where(has_one, weight(away0, slot0 > middle), 0)
        weight1 = jnp.where(has_two, weight(away1, slot1 > middle), 0)
        sign0 = jnp.where(slot0 > middle, -1, 1)
        sign1 = jnp.where(slot1 > middle, -1, 1)
        for u in range(band):
            in0 = u < weight0
            in1 = u < weight0 + weight1
            step = jnp.where(in0, u, u - weight0)
            away = jnp.where(in0, away0, away1)
            sign = jnp.where(in0, sign0, sign1)
            same = step < middle + 1 - away
            move = jnp.where(same, step, -(step - middle + 2 * away))
            row = jnp.where(in0, row0, row1)
            slot = jnp.where(in1, middle + sign * move, middle)
            used = in1 & (owner_of[row * slots + slot] >= 0)
            send[peer, u] = jnp.where(used, loc[row, slot], zero_block)
        key0 = cl[slot0, first + row0] * slots + slots - 1 - slot0
        key1 = cl[slot1, first + row1] * slots + slots - 1 - slot1
        swap = has_two & (key1 < key0)
        first_code[peer] = jnp.where(swap, code1, code0)
        first_weight[peer] = jnp.where(
            swap, weight(away1, slot1 < middle), weight(away0, slot0 < middle)
        )

    @pl.loop(0, early)
    def _(j):
        fill(peer_of(in_turn(j)))

    pl.semaphore_wait(barrier, owners - 1 + 3)

    @pl.loop(0, early)
    def _(j):
        peer = peer_of(in_turn(j))
        band_copy(peer, me, peer).start()

    @pl.loop(early, owners - 1)
    def _(j):
        peer = peer_of(in_turn(j))
        fill(peer)
        band_copy(peer, me, peer).start()

    first_code[me] = 0
    first_weight[me] = 0

    blocks_copy.wait()

    @pl.loop(0, rows)
    def _(k):
        for b in range(slots):
            n = k * slots + b
            present = cl[b, first + k] >= 0
            block = blocks[k, b]
            block = jnp.where(present, block, jnp.zeros_like(block))
            own[k, b * size : (b + 1) * size, :] = block.T
            value = jnp.where(present, loc[k, b], zero_block)
            tab[local_at + n] = value
            if b != middle:
                win[k, middle * strip : (middle + 1) * strip, b * size : (b + 1) * size] = value
        for b in range(slots):
            value = own[k, pl.ds(pl.multiple_of(b * size + part * strip, strip), strip), :]
            tab[turn_at + local_at + k * slots + b] = value
            win[k, b * strip : (b + 1) * strip, middle * size : (middle + 1) * size] = value

    running = jnp.int32(0)
    for i in range(rows):
        for a in range(slots):
            n = i * slots + a
            column = cl[a, first + i]
            absent = column < 0
            column = jnp.where(absent, first + i, column)
            owner = column // rows
            running = running + jnp.where(owner == me, 0, 1)
            cum[n] = running
            where_sent[n] = jnp.where(
                owner == me,
                i * rows + column - first,
                jnp.minimum(crossing_at + running - 1, most - 1),
            )
            is_local[n] = jnp.where(owner == me, 1, 0)
            remote_base[n] = owner * pad + jnp.where(first_code[owner] == n, 0, first_weight[owner])
            local_base[n] = local_at + (column - first) * slots

    @pl.loop(0, rows)
    def _(i):
        for a in range(slots):
            for s in range(slots):
                if a == middle or s == middle or abs(a - s) > middle:
                    continue
                away_a, away_s = a - middle, s - middle
                direct = sends(away_s, away_a)
                edge, other = (s, a) if direct else (a, s)
                away_e, away_o = (away_s, away_a) if direct else (away_a, away_s)
                if (away_e > 0) == (away_o > 0):
                    u = abs(away_o) - abs(away_e)
                else:
                    u = middle - abs(away_e) + abs(away_o)
                n = i * slots + edge
                entry = jnp.where(
                    is_local[n] == 1, local_base[n] + (other - edge + middle), remote_base[n] + u
                )
                entries[(i * slots + a) * slots + s] = entry + (0 if direct else turn_at)

    @pl.loop(0, rows)
    def _(k):
        for a in range(slots):
            for s in range(slots):
                if abs(a - s) > middle:
                    win[k, s * strip : (s + 1) * strip, a * size : (a + 1) * size] = zero_block

    wide = parts * size
    line = lax.broadcasted_iota(jnp.int32, (wide, wide), 0)
    from_part, from_block, from_row = line // size, (line % size) // strip, line % strip
    shuffle[...] = (
        lax.broadcasted_iota(jnp.int32, (wide, wide), 1)
        == from_block * size + from_part * strip + from_row
    ).astype(jnp.bfloat16)

    def piece_copy(kind, batch, start):
        begin, end = batches[batch]
        span = pl.ds(begin * groups, (end - begin) * groups)
        other = partners[kind]
        return pltpu.make_async_remote_copy(
            src_ref=turned.at[other, span],
            dst_ref=pieces.at[part if start else other, span],
            send_sem=xsend_sem.at[kind, batch],
            recv_sem=xrecv_sem.at[kind, batch],
            device_id={"cols": other},
            device_id_type=MESH,
        )

    for batch, (begin, end) in enumerate(batches):

        @pl.loop(begin, end)
        def _(j):
            peer = peer_of(j)
            band_copy(peer, peer, peer).wait_recv()

        @pl.loop(begin, end, unroll=min(end - begin, 4))
        def _(j):
            peer = peer_of(j)
            for g in range(groups):
                stack = jnp.concatenate([tab[peer * pad + g * parts + n] for n in range(parts)], 0)
                flipped = stack.T
                for c in range(parts):
                    turned[c, j * groups + g] = flipped[c * strip : (c + 1) * strip]
                pieces[part, j * groups + g] = turned[part, j * groups + g]

        for kind in range(3):
            piece_copy(kind, batch, True).start()

        if batch == 0:
            for i in range(rows):
                for k in range(rows):
                    entry = jnp.int32(count)
                    for a in range(slots):
                        entry = jnp.where(cl[a, first + i] == first + k, i * slots + a, entry)
                    source[i * rows + k] = entry

            @pl.loop(0, most - crossing_at)
            def _(t):
                entry = jnp.int32(0)
                for n in range(count):
                    entry = entry + jnp.where(cum[n] <= t, 1, 0)
                source[crossing_at + t] = entry

    for batch, (begin, end) in enumerate(batches):
        for kind in range(3):
            piece_copy(kind, batch, False).wait_recv()

        for c in range(parts):
            lanes = slice(c * size, (c + 1) * size)
            for g in range(begin * groups, end * groups):
                joined[g * strip : (g + 1) * strip, lanes] = pieces[c, g]
        spread = jnp.dot(
            joined[begin * groups * strip : end * groups * strip, :], shuffle[...],
            preferred_element_type=jnp.float32,
        ).astype(jnp.bfloat16)
        for j in range(begin, end):
            at = turn_at + peer_of(j) * pad
            for g in range(groups):
                top = ((j - begin) * groups + g) * strip
                for n in range(parts):
                    tab[at + g * parts + n] = spread[top : top + strip, n * size : (n + 1) * size]

    spans = [(i * rows, rows) for i in range(rows)]
    spans += [(crossing_at + q * chunk, chunk) for q in range(CHUNKS)]

    def strip_copy(src, dst, which, piece, peer, sem):
        span = pl.ds(*spans[piece])
        return pltpu.make_async_remote_copy(
            src_ref=src.at[which, span],
            dst_ref=dst.at[which, span],
            send_sem=csend_sem.at[sem, piece],
            recv_sem=crecv_sem.at[sem, piece],
            device_id={"cols": peer},
            device_id_type=MESH,
        )

    def to_across(piece):
        return strip_copy(near, away, low, piece, across, 0)

    def to_sibling(piece, which):
        return strip_copy(near, near, which, piece, sibling, 1)

    def forward(piece, which):
        return strip_copy(away, away, which, piece, sibling, 2)

    def send_strips(piece):
        begin, length = spans[piece]
        for t in range(begin, begin + length):
            near[low, t] = sq[source[t]]
        to_across(piece).start()
        to_sibling(piece, low).start()

    def build(i):
        for a in range(slots):
            for s in range(slots):
                if a == middle or s == middle or abs(a - s) > middle:
                    continue
                win[i, s * strip : (s + 1) * strip, a * size : (a + 1) * size] = tab[
                    entries[(i * slots + a) * slots + s]
                ]

    build(0)
    for i in range(rows):
        if i + 1 < rows:
            build(i + 1)
        total = jnp.dot(win[i], own[i], preferred_element_type=jnp.float32)
        for s in range(slots):
            value = total[s * strip : (s + 1) * strip]
            value = jnp.where(cl[s, first + i] >= 0, value, 0.0)
            sq[i * slots + s] = value.astype(jnp.bfloat16)
        send_strips(i)
    for piece in range(rows, len(spans)):
        send_strips(piece)

    wide_half = size // 2
    for i in range(rows):
        for a in range(0, slots, 2):
            lanes = slice(a * wide_half, a * wide_half + size)
            left = win[i, :, a * size : (a + 1) * size]
            if a + 1 < slots:
                right = win[i, :, (a + 1) * size : (a + 2) * size]
            else:
                right = jnp.zeros_like(left)
            for h in range(2):
                cut = slice(h * wide_half, (h + 1) * wide_half)
                halves[h, i, :, lanes] = jnp.concatenate([left[:, cut], right[:, cut]], 1)

    def stack_half(i, strips):
        for a in range(slots + slots % 2):
            top = a * wide_half
            for c in range(2):
                if a < slots:
                    value = strips[c, where_sent[i * slots + a]]
                    value = jnp.where(cl[a, first + i] >= 0, value, zero_block)
                else:
                    value = zero_block
                full[i, top + c * strip : top + (c + 1) * strip, :] = value

    for piece in range(len(spans)):
        to_sibling(piece, 1 - low).wait_recv()
    for i in range(rows):
        stack_half(i, near)
        partial[i] = jnp.dot(halves[high, i], full[i], preferred_element_type=jnp.float32)

    for piece in range(len(spans)):
        to_across(piece).wait_recv()
        forward(piece, low).start()
    for piece in range(len(spans)):
        forward(piece, 1 - low).wait_recv()

    for i in range(rows):
        stack_half(i, away)
        total = partial[i] + jnp.dot(
            halves[1 - high, i], full[i], preferred_element_type=jnp.float32
        )
        for s in range(slots):
            value = 3.0 * sq[i * slots + s].astype(jnp.float32) - 2.0 * total[s * strip : (s + 1) * strip]
            value = jnp.where(cl[s, first + i] >= 0, value, 0.0)
            out[i, s] = value.astype(jnp.bfloat16)

    @pl.loop(0, owners - 1)
    def _(j):
        peer = peer_of(j)
        band_copy(peer, me, peer).wait_send()

    for batch in range(len(batches)):
        for kind in range(3):
            piece_copy(kind, batch, True).wait_send()

    for piece in range(len(spans)):
        to_across(piece).wait_send()
        to_sibling(piece, low).wait_send()
        forward(piece, low).wait_send()


def body(column_lists, block_values):
    rows, slots, size, _ = block_values.shape
    owners = lax.axis_size("rows")
    parts = lax.axis_size("cols")
    assert parts == 4
    strip = size // parts
    middle = (slots - 1) // 2
    band = middle + 1
    pad = -(-band // parts) * parts
    groups = pad // parts
    peers = owners - 1
    half_sum = (slots + slots % 2) * size // 2
    count = rows * slots
    crossing = min(count - rows, CAP * peers)
    most = rows * rows + -(-crossing // CHUNKS) * CHUNKS
    bf16 = jnp.bfloat16
    table = 2 * (owners * pad + count)
    result = pl.pallas_call(
        functools.partial(kernel, owners, rows, slots, size, strip, band, pad, most),
        out_shape=jax.ShapeDtypeStruct((rows, slots, strip, size), bf16),
        in_specs=[pl.BlockSpec(memory_space=pl.ANY), pl.BlockSpec(memory_space=pl.ANY)],
        out_specs=pl.BlockSpec(memory_space=pltpu.VMEM),
        scratch_shapes=[
            pltpu.SMEM(column_lists.shape[::-1], jnp.int32),
            pltpu.VMEM(block_values.shape, bf16),
            pltpu.VMEM((rows, slots, strip, size), bf16),
            pltpu.VMEM((owners, band, strip, size), bf16),
            pltpu.VMEM((table, strip, size), bf16),
            pltpu.VMEM((rows, slots * strip, slots * size), bf16),
            pltpu.VMEM((rows, slots * size, size), bf16),
            pltpu.VMEM((count + 1, strip, size), bf16),
            pltpu.VMEM((2, most, strip, size), bf16),
            pltpu.VMEM((2, most, strip, size), bf16),
            pltpu.VMEM((rows, half_sum, size), bf16),
            pltpu.VMEM((2, rows, slots * strip, half_sum), bf16),
            pltpu.VMEM((rows, slots * strip, size), jnp.float32),
            pltpu.VMEM((parts, peers * groups, strip, size), bf16),
            pltpu.VMEM((parts, peers * groups, strip, size), bf16),
            pltpu.VMEM((peers * groups * strip, parts * size), bf16),
            pltpu.VMEM((parts * size, parts * size), bf16),
            pltpu.SMEM((count,), jnp.int32),
            pltpu.SMEM((owners,), jnp.int32),
            pltpu.SMEM((owners,), jnp.int32),
            pltpu.SMEM((count,), jnp.int32),
            pltpu.SMEM((count,), jnp.int32),
            pltpu.SMEM((count,), jnp.int32),
            pltpu.SMEM((count * slots,), jnp.int32),
            pltpu.SMEM((count,), jnp.int32),
            pltpu.SMEM((count,), jnp.int32),
            pltpu.SMEM((most,), jnp.int32),
            pltpu.SemaphoreType.DMA((owners,)),
            pltpu.SemaphoreType.DMA((owners,)),
            pltpu.SemaphoreType.DMA((3, BATCHES)),
            pltpu.SemaphoreType.DMA((3, BATCHES)),
            pltpu.SemaphoreType.DMA((3, rows + CHUNKS)),
            pltpu.SemaphoreType.DMA((3, rows + CHUNKS)),
            pltpu.SemaphoreType.DMA((3,)),
        ],
        compiler_params=pltpu.CompilerParams(
            collective_id=0, has_side_effects=True, vmem_limit_bytes=52 * 1024 * 1024
        ),
    )(column_lists.T, block_values)
    return jnp.swapaxes(result, 2, 3)


def solution(mesh):
    in_specs = (P(), P("rows", None, None, None))
    out_specs = P("rows", None, None, "cols")
    return jax.shard_map(body, mesh=mesh, in_specs=in_specs, out_specs=out_specs, check_vma=False)
```

```python
import functools

import jax
import jax.numpy as jnp
from jax import lax
from jax.experimental import pallas as pl
from jax.experimental.pallas import tpu as pltpu
from jax.sharding import PartitionSpec as P

CAP = 2
CHUNKS = 2
BATCHES = 4
MESH = pl.DeviceIdType.MESH


def sends(offset, other):
    if (offset > 0) == (other > 0):
        return abs(other) >= abs(offset)
    return abs(other) < abs(offset) or (abs(other) == abs(offset) and offset > 0)


def kernel(
    owners, rows, slots, size, strip, band, pad, most,
    cl_hbm, blocks_hbm, out,
    cl, blocks, loc, send, tab, win, own, sq, near, away, full, halves, partial, turned, pieces, joined, shuffle,
    owner_of, first_code, first_weight, remote_base, local_base, is_local, entries, cum, where_sent, source,
    send_sem, recv_sem, xsend_sem, xrecv_sem, csend_sem, crecv_sem, in_sem,
):
    middle = (slots - 1) // 2
    count = rows * slots
    parts = size // strip
    me = lax.axis_index("rows")
    part = lax.axis_index("cols")
    high, low = part // 2, part % 2
    sibling = high * 2 + (1 - low)
    across = (1 - high) * 2 + low
    far = (1 - high) * 2 + (1 - low)
    partners = (across, far, sibling)
    first = me * rows
    local_at = owners * pad
    turn_at = local_at + count
    chunk = (most - rows * rows) // CHUNKS
    groups = pad // parts
    bounds = [0, owners // 2 - 1, 3 * owners // 4 - 1, 7 * owners // 8 - 1, owners - 1]
    batches = list(zip(bounds[:-1], bounds[1:]))
    early = 1
    crossing_at = rows * rows
    part_rows = pl.ds(pl.multiple_of(part * strip, strip), strip)

    def peer_of(j):
        peer, bit = 0, 1
        while bit < owners:
            peer = peer + ((me // bit + (j + 1) // bit) % 2) * bit
            bit *= 2
        return peer

    def in_turn(j):
        return (j // 2 + owners // 2) * (1 - j % 2) + ((j + 1) // 2) * (j % 2) - 1

    cl_copy = pltpu.make_async_copy(cl_hbm, cl, in_sem.at[0])
    loc_copy = pltpu.make_async_copy(blocks_hbm.at[:, :, part_rows, :], loc, in_sem.at[2])
    blocks_copy = pltpu.make_async_copy(blocks_hbm, blocks, in_sem.at[1])
    cl_copy.start()
    loc_copy.start()
    blocks_copy.start()

    barrier = pltpu.get_barrier_semaphore()

    @pl.loop(0, owners - 1)
    def _(j):
        pl.semaphore_signal(barrier, inc=1, device_id={"rows": peer_of(j)}, device_id_type=MESH)

    for other in partners:
        pl.semaphore_signal(barrier, inc=1, device_id={"cols": other}, device_id_type=MESH)

    zero_block = jnp.zeros((strip, size), jnp.bfloat16)
    sq[count] = zero_block

    @pl.loop(0, owners)
    def _(o):
        for u in range(band, pad):
            tab[o * pad + u] = zero_block

    cl_copy.wait()
    for k in range(rows):
        for b in range(slots):
            column = cl[b, first + k]
            owner_of[k * slots + b] = jnp.where(column >= 0, jnp.maximum(column, 0) // rows, -1)
    loc_copy.wait()

    def band_copy(src, dst_owner, peer):
        return pltpu.make_async_remote_copy(
            src_ref=send.at[src],
            dst_ref=tab.at[pl.ds(dst_owner * pad, band)],
            send_sem=send_sem.at[src],
            recv_sem=recv_sem.at[dst_owner],
            device_id={"rows": peer},
            device_id_type=MESH,
        )

    def weight(distance, negative):
        return middle + 1 - distance + jnp.minimum(
            distance - jnp.where(negative, 1, 0), middle - distance
        )

    def fill(peer):
        lowest = jnp.int32(count)
        highest = jnp.int32(-1)
        for n in range(count):
            hit = owner_of[n] == peer
            lowest = jnp.minimum(lowest, jnp.where(hit, n, count))
            highest = jnp.maximum(highest, jnp.where(hit, n, -1))
        has_one = highest >= 0
        has_two = highest > lowest
        code0 = jnp.where(has_one, lowest, 0)
        code1 = jnp.where(has_two, highest, 0)
        row0, row1 = code0 // slots, code1 // slots
        slot0, slot1 = code0 - row0 * slots, code1 - row1 * slots
        away0, away1 = jnp.abs(slot0 - middle), jnp.abs(slot1 - middle)
        weight0 = jnp.where(has_one, weight(away0, slot0 > middle), 0)
        weight1 = jnp.where(has_two, weight(away1, slot1 > middle), 0)
        sign0 = jnp.where(slot0 > middle, -1, 1)
        sign1 = jnp.where(slot1 > middle, -1, 1)
        for u in range(band):
            in0 = u < weight0
            in1 = u < weight0 + weight1
            step = jnp.where(in0, u, u - weight0)
            away = jnp.where(in0, away0, away1)
            sign = jnp.where(in0, sign0, sign1)
            same = step < middle + 1 - away
            move = jnp.where(same, step, -(step - middle + 2 * away))
            row = jnp.where(in0, row0, row1)
            slot = jnp.where(in1, middle + sign * move, middle)
            used = in1 & (owner_of[row * slots + slot] >= 0)
            send[peer, u] = jnp.where(used, loc[row, slot], zero_block)
        key0 = cl[slot0, first + row0] * slots + slots - 1 - slot0
        key1 = cl[slot1, first + row1] * slots + slots - 1 - slot1
        swap = has_two & (key1 < key0)
        first_code[peer] = jnp.where(swap, code1, code0)
        first_weight[peer] = jnp.where(
            swap, weight(away1, slot1 < middle), weight(away0, slot0 < middle)
        )

    @pl.loop(0, early)
    def _(j):
        fill(peer_of(in_turn(j)))

    pl.semaphore_wait(barrier, owners - 1 + 3)

    @pl.loop(0, early)
    def _(j):
        peer = peer_of(in_turn(j))
        band_copy(peer, me, peer).start()

    @pl.loop(early, owners - 1)
    def _(j):
        peer = peer_of(in_turn(j))
        fill(peer)
        band_copy(peer, me, peer).start()

    first_code[me] = 0
    first_weight[me] = 0

    blocks_copy.wait()

    @pl.loop(0, rows)
    def _(k):
        for b in range(slots):
            n = k * slots + b
            present = cl[b, first + k] >= 0
            block = blocks[k, b]
            block = jnp.where(present, block, jnp.zeros_like(block))
            own[k, b * size : (b + 1) * size, :] = block.T
            value = jnp.where(present, loc[k, b], zero_block)
            tab[local_at + n] = value
            if b != middle:
                win[k, middle * strip : (middle + 1) * strip, b * size : (b + 1) * size] = value
        for b in range(slots):
            value = own[k, pl.ds(pl.multiple_of(b * size + part * strip, strip), strip), :]
            tab[turn_at + local_at + k * slots + b] = value
            win[k, b * strip : (b + 1) * strip, middle * size : (middle + 1) * size] = value

    running = jnp.int32(0)
    for i in range(rows):
        for a in range(slots):
            n = i * slots + a
            column = cl[a, first + i]
            absent = column < 0
            column = jnp.where(absent, first + i, column)
            owner = column // rows
            running = running + jnp.where(owner == me, 0, 1)
            cum[n] = running
            where_sent[n] = jnp.where(
                owner == me,
                i * rows + column - first,
                jnp.minimum(crossing_at + running - 1, most - 1),
            )
            is_local[n] = jnp.where(owner == me, 1, 0)
            remote_base[n] = owner * pad + jnp.where(first_code[owner] == n, 0, first_weight[owner])
            local_base[n] = local_at + (column - first) * slots

    @pl.loop(0, rows)
    def _(i):
        for a in range(slots):
            for s in range(slots):
                if a == middle or s == middle or abs(a - s) > middle:
                    continue
                away_a, away_s = a - middle, s - middle
                direct = sends(away_s, away_a)
                edge, other = (s, a) if direct else (a, s)
                away_e, away_o = (away_s, away_a) if direct else (away_a, away_s)
                if (away_e > 0) == (away_o > 0):
                    u = abs(away_o) - abs(away_e)
                else:
                    u = middle - abs(away_e) + abs(away_o)
                n = i * slots + edge
                entry = jnp.where(
                    is_local[n] == 1, local_base[n] + (other - edge + middle), remote_base[n] + u
                )
                entries[(i * slots + a) * slots + s] = entry + (0 if direct else turn_at)

    @pl.loop(0, rows)
    def _(k):
        for a in range(slots):
            for s in range(slots):
                if abs(a - s) > middle:
                    win[k, s * strip : (s + 1) * strip, a * size : (a + 1) * size] = zero_block

    wide = parts * size
    line = lax.broadcasted_iota(jnp.int32, (wide, wide), 0)
    from_part, from_block, from_row = line // size, (line % size) // strip, line % strip
    shuffle[...] = (
        lax.broadcasted_iota(jnp.int32, (wide, wide), 1)
        == from_block * size + from_part * strip + from_row
    ).astype(jnp.bfloat16)

    def piece_copy(kind, batch, start):
        begin, end = batches[batch]
        span = pl.ds(begin * groups, (end - begin) * groups)
        other = partners[kind]
        return pltpu.make_async_remote_copy(
            src_ref=turned.at[other, span],
            dst_ref=pieces.at[part if start else other, span],
            send_sem=xsend_sem.at[kind, batch],
            recv_sem=xrecv_sem.at[kind, batch],
            device_id={"cols": other},
            device_id_type=MESH,
        )

    for batch, (begin, end) in enumerate(batches):

        @pl.loop(begin, end)
        def _(j):
            peer = peer_of(j)
            band_copy(peer, peer, peer).wait_recv()

        @pl.loop(begin, end, unroll=min(end - begin, 4))
        def _(j):
            peer = peer_of(j)
            for g in range(groups):
                stack = jnp.concatenate([tab[peer * pad + g * parts + n] for n in range(parts)], 0)
                flipped = stack.T
                for c in range(parts):
                    turned[c, j * groups + g] = flipped[c * strip : (c + 1) * strip]
                pieces[part, j * groups + g] = turned[part, j * groups + g]

        for kind in range(3):
            piece_copy(kind, batch, True).start()

        if batch == 0:
            for i in range(rows):
                for k in range(rows):
                    entry = jnp.int32(count)
                    for a in range(slots):
                        entry = jnp.where(cl[a, first + i] == first + k, i * slots + a, entry)
                    source[i * rows + k] = entry

            @pl.loop(0, most - crossing_at)
            def _(t):
                entry = jnp.int32(0)
                for n in range(count):
                    entry = entry + jnp.where(cum[n] <= t, 1, 0)
                source[crossing_at + t] = entry

    for batch, (begin, end) in enumerate(batches):
        for kind in range(3):
            piece_copy(kind, batch, False).wait_recv()

        for c in range(parts):
            lanes = slice(c * size, (c + 1) * size)
            for g in range(begin * groups, end * groups):
                joined[g * strip : (g + 1) * strip, lanes] = pieces[c, g]
        spread = jnp.dot(
            joined[begin * groups * strip : end * groups * strip, :], shuffle[...],
            preferred_element_type=jnp.float32,
        ).astype(jnp.bfloat16)
        for j in range(begin, end):
            at = turn_at + peer_of(j) * pad
            for g in range(groups):
                top = ((j - begin) * groups + g) * strip
                for n in range(parts):
                    tab[at + g * parts + n] = spread[top : top + strip, n * size : (n + 1) * size]

    spans = [(i * rows, rows) for i in range(rows)]
    spans += [(crossing_at + q * chunk, chunk) for q in range(CHUNKS)]

    def strip_copy(src, dst, which, piece, peer, sem):
        span = pl.ds(*spans[piece])
        return pltpu.make_async_remote_copy(
            src_ref=src.at[which, span],
            dst_ref=dst.at[which, span],
            send_sem=csend_sem.at[sem, piece],
            recv_sem=crecv_sem.at[sem, piece],
            device_id={"cols": peer},
            device_id_type=MESH,
        )

    def to_across(piece):
        return strip_copy(near, away, low, piece, across, 0)

    def to_sibling(piece, which):
        return strip_copy(near, near, which, piece, sibling, 1)

    def forward(piece, which):
        return strip_copy(away, away, which, piece, sibling, 2)

    def send_strips(piece):
        begin, length = spans[piece]
        for t in range(begin, begin + length):
            near[low, t] = sq[source[t]]
        to_across(piece).start()
        to_sibling(piece, low).start()

    def build(i):
        for a in range(slots):
            for s in range(slots):
                if a == middle or s == middle or abs(a - s) > middle:
                    continue
                win[i, s * strip : (s + 1) * strip, a * size : (a + 1) * size] = tab[
                    entries[(i * slots + a) * slots + s]
                ]

    build(0)
    for i in range(rows):
        if i + 1 < rows:
            build(i + 1)
        total = jnp.dot(win[i], own[i], preferred_element_type=jnp.float32)
        for s in range(slots):
            value = total[s * strip : (s + 1) * strip]
            value = jnp.where(cl[s, first + i] >= 0, value, 0.0)
            sq[i * slots + s] = value.astype(jnp.bfloat16)
        send_strips(i)
    for piece in range(rows, len(spans)):
        send_strips(piece)

    wide_half = size // 2
    for i in range(rows):
        for a in range(0, slots, 2):
            lanes = slice(a * wide_half, a * wide_half + size)
            left = win[i, :, a * size : (a + 1) * size]
            if a + 1 < slots:
                right = win[i, :, (a + 1) * size : (a + 2) * size]
            else:
                right = jnp.zeros_like(left)
            for h in range(2):
                cut = slice(h * wide_half, (h + 1) * wide_half)
                halves[h, i, :, lanes] = jnp.concatenate([left[:, cut], right[:, cut]], 1)

    def stack_half(i, strips):
        for a in range(slots + slots % 2):
            top = a * wide_half
            for c in range(2):
                if a < slots:
                    value = strips[c, where_sent[i * slots + a]]
                    value = jnp.where(cl[a, first + i] >= 0, value, zero_block)
                else:
                    value = zero_block
                full[i, top + c * strip : top + (c + 1) * strip, :] = value

    for piece in range(len(spans)):
        to_sibling(piece, 1 - low).wait_recv()
    for i in range(rows):
        stack_half(i, near)
        partial[i] = jnp.dot(halves[high, i], full[i], preferred_element_type=jnp.float32)

    for piece in range(len(spans)):
        to_across(piece).wait_recv()
        forward(piece, low).start()
    for piece in range(len(spans)):
        forward(piece, 1 - low).wait_recv()

    for i in range(rows):
        stack_half(i, away)
        total = partial[i] + jnp.dot(
            halves[1 - high, i], full[i], preferred_element_type=jnp.float32
        )
        for s in range(slots):
            value = 3.0 * sq[i * slots + s].astype(jnp.float32) - 2.0 * total[s * strip : (s + 1) * strip]
            value = jnp.where(cl[s, first + i] >= 0, value, 0.0)
            out[i, s] = value.astype(jnp.bfloat16)

    @pl.loop(0, owners - 1)
    def _(j):
        peer = peer_of(j)
        band_copy(peer, me, peer).wait_send()

    for batch in range(len(batches)):
        for kind in range(3):
            piece_copy(kind, batch, True).wait_send()

    for piece in range(len(spans)):
        to_across(piece).wait_send()
        to_sibling(piece, low).wait_send()
        forward(piece, low).wait_send()


def body(column_lists, block_values):
    rows, slots, size, _ = block_values.shape
    owners = lax.axis_size("rows")
    parts = lax.axis_size("cols")
    assert parts == 4
    strip = size // parts
    middle = (slots - 1) // 2
    band = middle + 1
    pad = -(-band // parts) * parts
    groups = pad // parts
    peers = owners - 1
    half_sum = (slots + slots % 2) * size // 2
    count = rows * slots
    crossing = min(count - rows, CAP * peers)
    most = rows * rows + -(-crossing // CHUNKS) * CHUNKS
    bf16 = jnp.bfloat16
    table = 2 * (owners * pad + count)
    result = pl.pallas_call(
        functools.partial(kernel, owners, rows, slots, size, strip, band, pad, most),
        out_shape=jax.ShapeDtypeStruct((rows, slots, strip, size), bf16),
        in_specs=[pl.BlockSpec(memory_space=pl.ANY), pl.BlockSpec(memory_space=pl.ANY)],
        out_specs=pl.BlockSpec(memory_space=pltpu.VMEM),
        scratch_shapes=[
            pltpu.SMEM(column_lists.shape[::-1], jnp.int32),
            pltpu.VMEM(block_values.shape, bf16),
            pltpu.VMEM((rows, slots, strip, size), bf16),
            pltpu.VMEM((owners, band, strip, size), bf16),
            pltpu.VMEM((table, strip, size), bf16),
            pltpu.VMEM((rows, slots * strip, slots * size), bf16),
            pltpu.VMEM((rows, slots * size, size), bf16),
            pltpu.VMEM((count + 1, strip, size), bf16),
            pltpu.VMEM((2, most, strip, size), bf16),
            pltpu.VMEM((2, most, strip, size), bf16),
            pltpu.VMEM((rows, half_sum, size), bf16),
            pltpu.VMEM((2, rows, slots * strip, half_sum), bf16),
            pltpu.VMEM((rows, slots * strip, size), jnp.float32),
            pltpu.VMEM((parts, peers * groups, strip, size), bf16),
            pltpu.VMEM((parts, peers * groups, strip, size), bf16),
            pltpu.VMEM((peers * groups * strip, parts * size), bf16),
            pltpu.VMEM((parts * size, parts * size), bf16),
            pltpu.SMEM((count,), jnp.int32),
            pltpu.SMEM((owners,), jnp.int32),
            pltpu.SMEM((owners,), jnp.int32),
            pltpu.SMEM((count,), jnp.int32),
            pltpu.SMEM((count,), jnp.int32),
            pltpu.SMEM((count,), jnp.int32),
            pltpu.SMEM((count * slots,), jnp.int32),
            pltpu.SMEM((count,), jnp.int32),
            pltpu.SMEM((count,), jnp.int32),
            pltpu.SMEM((most,), jnp.int32),
            pltpu.SemaphoreType.DMA((owners,)),
            pltpu.SemaphoreType.DMA((owners,)),
            pltpu.SemaphoreType.DMA((3, BATCHES)),
            pltpu.SemaphoreType.DMA((3, BATCHES)),
            pltpu.SemaphoreType.DMA((3, rows + CHUNKS)),
            pltpu.SemaphoreType.DMA((3, rows + CHUNKS)),
            pltpu.SemaphoreType.DMA((3,)),
        ],
        compiler_params=pltpu.CompilerParams(
            collective_id=0, has_side_effects=True, vmem_limit_bytes=52 * 1024 * 1024
        ),
    )(column_lists.T, block_values)
    return jnp.swapaxes(result, 2, 3)


def solution(mesh):
    in_specs = (P(), P("rows", None, None, None))
    out_specs = P("rows", None, None, "cols")
    return jax.shard_map(body, mesh=mesh, in_specs=in_specs, out_specs=out_specs, check_vma=False)
```
